128 devices in a mesh: rep: 4 (over y), wide: 32 (over z, x, core).
Axes of the slice: x: 4, y: 4, z: 4, core: 2. Of those that a mesh axis runs over, the one named last changes fastest.
Arguments:
- amplitudes: bfloat16 [8, 32, 512, 2560], P(None, None, ('rep', 'wide')), may hold values from -6 to 6
- integrals: bfloat16 [8, 768, 81920], P(None, 'rep', 'wide'), may hold values from -0.01953125 to 0.01953125
- live_pairs: int32 [8], replicated, may hold values from 256 to 512, as said below
Outputs:
- ladder: bfloat16 [8, 512, 768], P(None, ('rep', 'wide'))
The draws below stay inside these ranges and needn't reach their ends.
Inputs may be any that keep to these rules, and one draw needn't show every extreme that they name: `live_pairs`: rows of an irrep block at or beyond its count are padding; some irrep has all 512 pairs.
All inputs are finite; a program needn't handle non-finite values.
Results may differ from the reference program's by a relative error of at most 0.002.
Values may be sent and summed in bfloat16 or wider, within the bound.
A program may use at most 192 MiB of HBM per device.

```python
import jax
import jax.numpy as jnp
from jax import lax

IRREPS = 8
OCC_PAIRS = 512
CD_DEV = 2560
CD_BLOCKS = 32
CD_PAIRS = 81920
COLS = 768


def draw_live_pairs(key, part):
    key = jax.random.fold_in(key, 7)
    first, second = jax.random.split(key)
    counts = jax.random.randint(first, (IRREPS,), OCC_PAIRS // 2, OCC_PAIRS + 1)
    chosen = jax.random.randint(second, (), 0, IRREPS)
    slots = jnp.arange(IRREPS, dtype=jnp.int32)
    return jnp.where(slots == chosen, OCC_PAIRS, counts).astype(jnp.int32)


def strengthened(drawn, rng, source, target, blocks, factor):
    owner, partner = [(jnp.arange(drawn.shape[axis_at]) // (drawn.shape[axis_at] // blocks)).reshape([-1 if axis == axis_at else 1 for axis in range(drawn.ndim)]) for axis_at in (source, target)]
    chosen = jax.random.permutation(rng, blocks)[partner]
    strong = (owner == chosen) | (owner == (partner + blocks // 2) % blocks)
    return jnp.where(strong, factor * drawn, drawn)


def block_scale(stream_key, shape, shards, least, top_value):
    def one(position, blocks):
        heights = jax.random.uniform(jax.random.fold_in(jax.random.fold_in(stream_key, 6), position), (blocks,), jnp.float32, least / len(shards), top_value / len(shards))
        return jnp.repeat(jnp.exp(heights), shape[position] // blocks).reshape((-1,) + (1,) * (len(shape) - position - 1))

    level = one(*shards[0])
    for cut in shards[1:]:
        level = level * one(*cut)
    return level


def bell_draw(stream_key, dims, spread, limit, shards=(), kind=jnp.bfloat16):
    entries = jax.random.normal(stream_key, dims, jnp.float32) * spread
    if len(shards) > 0:
        entries = block_scale(stream_key, dims, shards, -0.22, 0.18) * entries
    return jnp.clip(entries, min=-limit, max=limit).astype(kind)


def noise_with(key, shape, spread, most, cuts, heavy, held_as=jnp.bfloat16):
    values = spread * jax.random.normal(key, shape, jnp.float32)
    if cuts:
        values = values * block_scale(key, shape, cuts, -0.22, 0.18)
    return jnp.clip(strengthened(values, jax.random.fold_in(key, 3), *heavy), -most, most).astype(held_as)


def setup_inputs(seed: int = 0) -> dict:
    seeds = jax.random.split(jax.random.key(seed), 4)
    return {
        "amplitudes": noise_with(seeds[0], (IRREPS, CD_BLOCKS, OCC_PAIRS, CD_DEV), 1.0, 6.0, ((2, 128),), (1, 2, 32, 2.75)),
        "integrals": bell_draw(seeds[1], (IRREPS, COLS, CD_PAIRS), CD_PAIRS ** -0.5, 0.01953125, ((1, 4), (2, 32))),
        "live_pairs": draw_live_pairs(jax.random.fold_in(seeds[3], 71), 0),
    }


def reference(amplitudes, integrals, live_pairs):
    def one_block(pair):
        left, right = pair
        rows = jnp.transpose(left, (1, 0, 2)).reshape(OCC_PAIRS, CD_PAIRS)
        return jnp.dot(rows, right.T, preferred_element_type=jnp.float32)

    product = lax.map(one_block, (amplitudes, integrals))
    index = jnp.arange(OCC_PAIRS, dtype=jnp.int32)
    keep = index[None, :] < live_pairs[:, None]
    return jnp.where(keep[:, :, None], product, jnp.zeros_like(product)).astype(jnp.bfloat16)
```

```python
import functools

import jax
import jax.numpy as jnp
from jax import lax
from jax.experimental import pallas as pl
from jax.experimental.pallas import tpu as pltpu
from jax.sharding import PartitionSpec as P

MESH = pl.DeviceIdType.MESH
MIB = 2**20


def ladder_kernel(reps, members, amp, integ, out, rows, relay, cols, part, landed, summed, placed,
                  b_send, b_recv, b_own, a_send, a_recv, y_send, y_recv, r_send, r_recv, o_send, o_recv):
    r, w = lax.axis_index("rep"), lax.axis_index("wide")
    up, down, across = (r + 1) % reps, (r + reps - 1) % reps, (r + 2) % reps
    cuts = integ.shape[1]
    owned = amp.shape[2]
    halves = amp.shape[0] // reps

    def irrep(behind, half):
        return (r + reps - behind) % reps + reps * half

    def remote(src, dst, send, recv, rep, member):
        return pltpu.make_async_remote_copy(
            src_ref=src, dst_ref=dst, send_sem=send, recv_sem=recv, device_id=(rep, member), device_id_type=MESH
        )

    def wait_for(ref, sem):
        pltpu.make_async_copy(ref, ref, sem).wait()

    def other(t):
        return (w + t) % members

    barrier = pltpu.get_barrier_semaphore()
    for rep in (up, down, across):
        pl.semaphore_signal(barrier, inc=1, device_id=(rep, w), device_id_type=MESH)

    def greet(t, carry):
        pl.semaphore_signal(barrier, inc=1, device_id=(r, other(t)), device_id_type=MESH)
        return carry

    lax.fori_loop(1, members, greet, 0)
    pl.semaphore_wait(barrier, members + 2)

    mine, theirs = pl.ds(0, cuts), pl.ds(cuts, cuts)

    def send_columns(half):
        remote(integ.at[irrep(3, half)], cols.at[half, 0, theirs], b_send.at[half, 0], b_recv.at[half, 0], up, w).start()
        remote(integ.at[irrep(2, half)], cols.at[half, 1, theirs], b_send.at[half, 1], b_recv.at[half, 1], down, w).start()

    def own_columns(half, role):
        return pltpu.make_async_copy(integ.at[irrep(role, half)], cols.at[half, role, mine], b_own.at[half, role])

    def arriving(behind, half):
        return rows.at[half, behind, 0] if behind < 2 else relay.at[half, behind - 2]

    def spread(behind, half):
        g, target = irrep(behind, half), arriving(behind, half)
        send, recv = a_send.at[half, behind], a_recv.at[half, behind]
        pltpu.make_async_copy(amp.at[g, w], target.at[w], recv).start()

        def one(t, carry):
            remote(amp.at[g, other(t)], target.at[w], send, recv, r, other(t)).start()
            return carry

        lax.fori_loop(1, members, one, 0)

    def arrived(behind, half):
        wait_for(arriving(behind, half), a_recv.at[half, behind])

    def along(src, half, role, slot, rep, index):
        return remote(src, rows.at[half, role, slot], y_send.at[half, index], y_recv.at[half, role, slot - 1], rep, w)

    def relay_rows(half):
        arrived(3, half)
        along(relay.at[half, 1], half, 0, 2, up, 0).start()
        arrived(2, half)
        along(relay.at[half, 0], half, 1, 2, down, 1).start()

    def exchange_rows(half):
        arrived(0, half)
        along(rows.at[half, 0, 0], half, 1, 1, up, 2).start()
        arrived(1, half)
        along(rows.at[half, 1, 0], half, 0, 1, down, 3).start()

    def took(half, role, slot):
        wait_for(rows.at[half, role, slot], y_recv.at[half, role, slot - 1])

    def forward_rows(half):
        took(half, 0, 2)
        along(rows.at[half, 0, 2], half, 1, 3, up, 4).start()
        took(half, 1, 2)
        along(rows.at[half, 1, 2], half, 0, 3, down, 5).start()

    def multiply(half, role, slot):
        left = rows[half, role, slot].reshape(members * owned, rows.shape[-1])
        product = lax.dot_general(
            left, cols[half, role], (((1,), (1,)), ((), ())), preferred_element_type=jnp.float32
        )
        part[half, role, :, slot] = product.reshape(members, owned, 2 * cuts)

    def give(half, role, slots, stage):
        send, recv = r_send.at[half, role, stage], r_recv.at[half, role, stage]
        pltpu.make_async_copy(part.at[half, role, w, slots], landed.at[half, role, w, slots], recv).start()

        def one(t, carry):
            remote(
                part.at[half, role, other(t), slots], landed.at[half, role, w, slots], send, recv, r, other(t)
            ).start()
            return carry

        lax.fori_loop(1, members, one, 0)

    def add_up(half, role, slots, stage):
        wait_for(landed.at[half, role, :, slots], r_recv.at[half, role, stage])
        summed[half, role, slots] = jnp.sum(landed[half, role, :, slots], axis=0)

    def hand_out(half, role, slots):
        g = irrep(role, half)
        place = {0: r, 1: (up, down)[role], 2: (down, up)[role], 3: across}
        for slot in slots:
            if slot == 0:
                placed[g, role] = summed[half, role, 0]
            else:
                remote(summed.at[half, role, slot], placed.at[g, role], o_send.at[half, role, slot - 1],
                       o_recv.at[half], place[slot], w).start()

    every, early, late = pl.ds(0, 4), pl.ds(0, 3), pl.ds(3, 1)

    send_columns(0)
    spread(3, 0)
    spread(2, 0)
    for half in range(halves):
        for role in range(2):
            own_columns(half, role).start()
    spread(0, 0)
    spread(1, 0)
    relay_rows(0)
    exchange_rows(0)
    send_columns(1)
    spread(3, 1)
    spread(2, 1)
    forward_rows(0)
    spread(0, 1)
    spread(1, 1)
    relay_rows(1)
    exchange_rows(1)

    def columns_ready(half, role):
        own_columns(half, role).wait()
        wait_for(cols.at[half, role, theirs], b_recv.at[half, role])

    for role in range(2):
        columns_ready(0, role)
        multiply(0, role, 0)
        multiply(0, role, 2)
        took(0, role, 1)
        multiply(0, role, 1)
    for role in range(2):
        took(0, role, 3)
        multiply(0, role, 3)
        give(0, role, every, 0)
    forward_rows(1)
    for role in range(2):
        columns_ready(1, role)
        multiply(1, role, 0)
        multiply(1, role, 2)
    for role in range(2):
        add_up(0, role, every, 0)
        hand_out(0, role, range(4))
    for role in range(2):
        took(1, role, 1)
        multiply(1, role, 1)
        give(1, role, early, 0)
    for role in range(2):
        add_up(1, role, early, 0)
        hand_out(1, role, range(3))
    for role in range(2):
        took(1, role, 3)
        multiply(1, role, 3)
        give(1, role, late, 1)
    for role in range(2):
        add_up(1, role, late, 1)
        hand_out(1, role, (3,))

    for half in range(halves):
        wait_for(placed.at[pl.ds(reps * half, reps - 1)], o_recv.at[half])
    out[...] = placed[...]

    for half in range(halves):
        for role in range(2):
            wait_for(cols.at[half, role, theirs], b_send.at[half, role])
            for slot in range(3):
                wait_for(summed.at[half, role, slot], o_send.at[half, role, slot])
        for behind in range(reps):
            wait_for(relay.at[half, 0, pl.ds(1, members - 1)], a_send.at[half, behind])
        for index in range(6):
            wait_for(rows.at[half, 0, 0], y_send.at[half, index])
    some = pl.ds(1, members - 1)
    for role in range(2):
        wait_for(landed.at[0, role, some, every], r_send.at[0, role, 0])
        wait_for(landed.at[1, role, some, early], r_send.at[1, role, 0])
        wait_for(landed.at[1, role, some, late], r_send.at[1, role, 1])


def per_device(reps, members, amplitudes, integrals, live_pairs):
    irreps, blocks, owned, depth = amplitudes.shape
    cuts = integrals.shape[1]
    halves = irreps // reps
    dma = pltpu.SemaphoreType.DMA
    f32, bf16 = jnp.float32, jnp.bfloat16
    pieces = pl.pallas_call(
        functools.partial(ladder_kernel, reps, members),
        out_shape=jax.ShapeDtypeStruct((irreps, 2, owned, 2 * cuts), f32),
        in_specs=[pl.BlockSpec(memory_space=pl.ANY)] * 2,
        out_specs=pl.BlockSpec(memory_space=pltpu.VMEM),
        scratch_shapes=[
            pltpu.VMEM((halves, 2, 4, members, owned, depth), bf16),
            pltpu.VMEM((halves, 2, members, owned, depth), bf16),
            pltpu.VMEM((halves, 2, 2 * cuts, depth), bf16),
            pltpu.VMEM((halves, 2, members, 4, owned, 2 * cuts), f32),
            pltpu.VMEM((halves, 2, members, 4, owned, 2 * cuts), f32),
            pltpu.VMEM((halves, 2, 4, owned, 2 * cuts), f32),
            pltpu.VMEM((irreps, 2, owned, 2 * cuts), f32),
            dma((halves, 2)), dma((halves, 2)), dma((halves, 2)),
            dma((halves, 4)), dma((halves, 4)),
            dma((halves, 6)), dma((halves, 2, 3)),
            dma((halves, 2, 2)), dma((halves, 2, 2)),
            dma((halves, 2, 3)), dma((halves,)),
        ],
        compiler_params=pltpu.CompilerParams(collective_id=0, has_side_effects=True, vmem_limit_bytes=52 * MIB),
        cost_estimate=pl.CostEstimate(
            flops=2 * irreps * owned * members * 4 * cuts * depth, bytes_accessed=26 * MIB, transcendentals=0
        ),
        name="ladder",
    )(amplitudes, integrals)

    quarters = []
    for g in range(irreps):
        found = {}
        for role in range(2):
            here = (g + role) % reps
            found[here] = pieces[g, role, :, :cuts]
            found[(here + (reps - 1, 1)[role]) % reps] = pieces[g, role, :, cuts:]
        quarters.append(jnp.concatenate([found[q] for q in range(reps)], axis=1))
    ladder = jnp.stack(quarters)
    index = (lax.axis_index("rep") * members + lax.axis_index("wide")) * owned + jnp.arange(owned, dtype=jnp.int32)
    keep = index[None, :] < live_pairs[:, None]
    return jnp.where(keep[:, :, None], ladder, jnp.zeros_like(ladder)).astype(jnp.bfloat16)


def solution(mesh):
    in_specs = (P(None, None, ("rep", "wide"), None), P(None, "rep", "wide"), P())
    out_specs = P(None, ("rep", "wide"), None)
    return jax.shard_map(
        functools.partial(per_device, mesh.shape["rep"], mesh.shape["wide"]),
        mesh=mesh, in_specs=in_specs, out_specs=out_specs, check_vma=False,
    )
```

```python
import functools

import jax
import jax.numpy as jnp
from jax import lax
from jax.experimental import pallas as pl
from jax.experimental.pallas import tpu as pltpu
from jax.sharding import PartitionSpec as P

MESH = pl.DeviceIdType.MESH
MIB = 2**20
GROUP = 8


def ladder_kernel(reps, members, live, amp, integ, out, rows, relay, cols, part, landed, summed, placed, direct,
                  b_send, b_recv, b_own, a_send, a_recv, y_send, y_recv, p_send, p_recv,
                  r_send, r_recv, l_send, l_recv, o_send, o_recv, d_send, d_recv):
    r, w = lax.axis_index("rep"), lax.axis_index("wide")
    up, down, across = (r + 1) % reps, (r + reps - 1) % reps, (r + 2) % reps
    groups = members // GROUP
    plane, seat = w // GROUP, w % GROUP
    cuts = integ.shape[1]
    owned, depth = amp.shape[2], amp.shape[3]
    halves = amp.shape[0] // reps
    beside = {1: (down, up), 2: (across, across), 3: (up, down)}

    def irrep(behind, half):
        return (r + reps - behind) % reps + reps * half

    def remote(src, dst, send, recv, rep, member):
        return pltpu.make_async_remote_copy(
            src_ref=src, dst_ref=dst, send_sem=send, recv_sem=recv, device_id=(rep, member), device_id_type=MESH
        )

    def wait_for(ref, sem):
        pltpu.make_async_copy(ref, ref, sem).wait()

    def other(t):
        return (w + t) % members

    def neighbour(t):
        return plane * GROUP + (seat + t) % GROUP

    barrier = pltpu.get_barrier_semaphore()

    def greet(rep, member):
        pl.semaphore_signal(barrier, inc=1, device_id=(rep, member), device_id_type=MESH)

    def greet_rep(t, carry):
        greet(r, other(t))
        return carry

    def greet_group(t, carry):
        greet(up, neighbour(t))
        greet(down, neighbour(t))
        return carry

    greet(across, w)
    lax.fori_loop(0, GROUP, greet_group, 0)
    lax.fori_loop(1, members, greet_rep, 0)
    pl.semaphore_wait(barrier, members + 2 * GROUP)

    mine, theirs = pl.ds(0, cuts), pl.ds(cuts, cuts)

    def send_columns(half):
        remote(integ.at[irrep(3, half)], cols.at[half, 0, theirs], b_send.at[half, 0], b_recv.at[half, 0], up, w).start()
        remote(integ.at[irrep(2, half)], cols.at[half, 1, theirs], b_send.at[half, 1], b_recv.at[half, 1], down, w).start()

    def own_columns(half, role):
        return pltpu.make_async_copy(integ.at[irrep(role, half)], cols.at[half, role, mine], b_own.at[half, role])

    def columns_ready(half):
        for role in range(2):
            own_columns(half, role).wait()
            wait_for(cols.at[half, role, theirs], b_recv.at[half, role])

    def arriving(behind, half):
        return rows.at[half, behind, 0] if behind < 2 else relay.at[half, behind - 2]

    def spread(behind, half):
        g, target = irrep(behind, half), arriving(behind, half)
        send, recv = a_send.at[half, behind], a_recv.at[half, behind]
        pltpu.make_async_copy(amp.at[g, w], target.at[w], recv).start()

        def one(t, carry):
            remote(amp.at[g, other(t)], target.at[w], send, recv, r, other(t)).start()
            return carry

        lax.fori_loop(1, members, one, 0)

    def arrived(behind, half):
        wait_for(arriving(behind, half), a_recv.at[half, behind])

    def along(src, half, role, slot, rep):
        return remote(src, rows.at[half, role, slot], y_send.at[half, role, slot - 1], y_recv.at[half, role, slot - 1],
                      rep, w)

    def relay_rows(half):
        arrived(3, half)
        along(relay.at[half, 1], half, 0, 1, up).start()
        arrived(2, half)
        along(relay.at[half, 0], half, 1, 1, down).start()

    def forward_rows(half):
        took(half, 0, 1)
        along(rows.at[half, 0, 1], half, 1, 2, up).start()
        took(half, 1, 1)
        along(rows.at[half, 1, 1], half, 0, 2, down).start()

    def exchange_rows(half):
        arrived(0, half)
        along(rows.at[half, 0, 0], half, 1, 3, up).start()
        arrived(1, half)
        along(rows.at[half, 1, 0], half, 0, 3, down).start()

    def took(half, role, slot):
        wait_for(rows.at[half, role, slot], y_recv.at[half, role, slot - 1])

    def sent(half, slot):
        for role in range(2):
            wait_for(rows.at[half, role, slot], y_send.at[half, role, slot - 1])

    def group_at(step):
        return pl.ds((plane + step) % groups * GROUP, GROUP)

    def exchange_piece(step):
        for role, rep in ((0, up), (1, down)):
            remote(rows.at[1, role, 0, group_at(step)], rows.at[1, 1 - role, 3, group_at(step)],
                   p_send.at[role, step], p_recv.at[1 - role, step], rep, w).start()

    def product(left, half, role):
        return lax.dot_general(left, cols[half, role], (((1,), (1,)), ((), ())), preferred_element_type=jnp.float32)

    def multiply(half, role, slot):
        left = rows[half, role, slot].reshape(members * owned, depth)
        part[half, role, :, slot] = product(left, half, role).reshape(members, owned, 2 * cuts)

    def multiply_piece(step):
        for role in range(2):
            at = group_at(step)
            wait_for(rows.at[1, role, 3, at], p_recv.at[role, step])
            left = rows[1, role, 3, at].reshape(GROUP * owned, depth)
            part[1, role, at, 3] = product(left, 1, role).reshape(GROUP, owned, 2 * cuts)

    def give(half, role, slots):
        send, recv = r_send.at[half, role], r_recv.at[half, role]
        pltpu.make_async_copy(part.at[half, role, w, slots], landed.at[half, role, w, slots], recv).start()

        def one(t, carry):
            remote(
                part.at[half, role, other(t), slots], landed.at[half, role, w, slots], send, recv, r, other(t)
            ).start()
            return carry

        lax.fori_loop(1, members, one, 0)

    def give_piece(step):
        base = (plane + step) % groups * GROUP

        def one(t, carry):
            member = base + (seat + t) % GROUP
            remote(part.at[1, :, member, 3], landed.at[1, :, step * GROUP + seat, 3], l_send, l_recv, r, member).start()
            return carry

        lax.fori_loop(0, GROUP, one, 0)

    def give_direct():
        def one(t, carry):
            for role in range(2):
                remote(part.at[1, role, neighbour(t), 3], direct.at[role, seat], d_send, d_recv,
                       beside[3][role], neighbour(t)).start()
            return carry

        lax.fori_loop(0, GROUP, one, 0)

    def add_up(half, role, slots):
        wait_for(landed.at[half, role, :, slots], r_recv.at[half, role])
        summed[half, role, slots] = jnp.sum(landed[half, role, :, slots], axis=0)

    far = pl.ds(GROUP, members - GROUP)

    def add_up_pieces():
        wait_for(landed.at[1, :, far, 3], l_recv)
        summed[1, :, 3] = jnp.sum(landed[1, :, far, 3], axis=1)

    def hand_out(half, role, slots):
        g = irrep(role, half)
        for slot in slots:
            if slot == 0:
                placed[g, role] = summed[half, role, 0]
            else:
                remote(summed.at[half, role, slot], placed.at[g, role], o_send.at[half, role, slot - 1],
                       o_recv.at[half], beside[slot][role], w).start()

    def finish(half):
        index = (r * members + w) * owned + lax.broadcasted_iota(jnp.int32, (owned, reps * cuts), 0)
        for p in range(reps):
            g = reps * half + p
            found = {}
            for role, beyond in ((0, reps - 1), (1, 1)):
                here = (p + role) % reps
                found[here] = placed[g, role, :, :cuts]
                found[(here + beyond) % reps] = placed[g, role, :, cuts:]
            ladder = jnp.concatenate([found[q] for q in range(reps)], axis=1)
            out[g] = jnp.where(index < live[g], ladder, 0.0).astype(out.dtype)

    every, early = pl.ds(0, 4), pl.ds(0, 3)

    send_columns(0)
    spread(3, 0)
    spread(2, 0)
    for half in range(halves):
        for role in range(2):
            own_columns(half, role).start()
    spread(3, 1)
    spread(2, 1)
    relay_rows(0)
    relay_rows(1)
    send_columns(1)
    spread(0, 0)
    spread(1, 0)
    spread(0, 1)
    spread(1, 1)
    forward_rows(0)
    exchange_rows(0)
    forward_rows(1)

    columns_ready(0)
    for role in range(2):
        multiply(0, role, 0)
        multiply(0, role, 1)
    for role in range(2):
        took(0, role, 2)
        multiply(0, role, 2)
    arrived(0, 1)
    arrived(1, 1)
    columns_ready(1)
    for role in range(2):
        multiply(1, role, 0)
        multiply(1, role, 1)
    sent(0, 3)
    exchange_piece(1)
    exchange_piece(2)
    for role in range(2):
        took(0, role, 3)
        multiply(0, role, 3)
        give(0, role, every)
    for role in range(2):
        add_up(0, role, every)
        hand_out(0, role, range(4))
    sent(1, 2)
    exchange_piece(3)
    exchange_piece(0)
    for role in range(2):
        took(1, role, 2)
        multiply(1, role, 2)
        give(1, role, early)
    multiply_piece(1)
    give_piece(1)
    for role in range(2):
        add_up(1, role, early)
        hand_out(1, role, range(3))
    multiply_piece(2)
    give_piece(2)
    wait_for(placed.at[pl.ds(0, reps - 1)], o_recv.at[0])
    finish(0)
    multiply_piece(3)
    give_piece(3)
    multiply_piece(0)
    give_direct()
    add_up_pieces()
    for role in range(2):
        hand_out(1, role, (3,))
    wait_for(direct, d_recv)
    wait_for(placed.at[pl.ds(reps, reps - 1)], o_recv.at[1])
    for role, behind in ((0, 1), (1, 0)):
        g = irrep(behind, 1)
        placed[g, role] = placed[g, role] + jnp.sum(direct[role], axis=0)
    finish(1)

    for half in range(halves):
        for role in range(2):
            wait_for(cols.at[half, role, theirs], b_send.at[half, role])
            for slot in range(3):
                wait_for(summed.at[half, role, slot], o_send.at[half, role, slot])
        for behind in range(reps):
            wait_for(relay.at[half, 0, pl.ds(1, members - 1)], a_send.at[half, behind])
        sent(half, 1)
    sent(0, 2)
    some = pl.ds(1, members - 1)
    for role in range(2):
        for step in range(groups):
            wait_for(rows.at[1, role, 0, group_at(step)], p_send.at[role, step])
        wait_for(landed.at[0, role, some, every], r_send.at[0, role])
        wait_for(landed.at[1, role, some, early], r_send.at[1, role])
    wait_for(landed.at[1, :, far, 3], l_send)
    wait_for(direct, d_send)


def per_device(reps, members, amplitudes, integrals, live_pairs):
    irreps, blocks, owned, depth = amplitudes.shape
    cuts = integrals.shape[1]
    halves = irreps // reps
    dma = pltpu.SemaphoreType.DMA
    f32, bf16 = jnp.float32, jnp.bfloat16
    return pl.pallas_call(
        functools.partial(ladder_kernel, reps, members),
        out_shape=jax.ShapeDtypeStruct((irreps, owned, reps * cuts), bf16),
        in_specs=[pl.BlockSpec(memory_space=pltpu.SMEM)] + [pl.BlockSpec(memory_space=pl.ANY)] * 2,
        out_specs=pl.BlockSpec(memory_space=pltpu.VMEM),
        scratch_shapes=[
            pltpu.VMEM((halves, 2, 4, members, owned, depth), bf16),
            pltpu.VMEM((halves, 2, members, owned, depth), bf16),
            pltpu.VMEM((halves, 2, 2 * cuts, depth), bf16),
            pltpu.VMEM((halves, 2, members, 4, owned, 2 * cuts), f32),
            pltpu.VMEM((halves, 2, members, 4, owned, 2 * cuts), f32),
            pltpu.VMEM((halves, 2, 4, owned, 2 * cuts), f32),
            pltpu.VMEM((irreps, 2, owned, 2 * cuts), f32),
            pltpu.VMEM((2, GROUP, owned, 2 * cuts), f32),
            dma((halves, 2)), dma((halves, 2)), dma((halves, 2)),
            dma((halves, 4)), dma((halves, 4)),
            dma((halves, 2, 3)), dma((halves, 2, 3)),
            dma((2, 4)), dma((2, 4)),
            dma((halves, 2)), dma((halves, 2)),
            dma, dma,
            dma((halves, 2, 3)), dma((halves,)),
            dma, dma,
        ],
        compiler_params=pltpu.CompilerParams(collective_id=0, has_side_effects=True, vmem_limit_bytes=52 * MIB),
        cost_estimate=pl.CostEstimate(
            flops=2 * irreps * owned * members * 4 * cuts * depth, bytes_accessed=26 * MIB, transcendentals=0
        ),
        name="ladder",
    )(live_pairs, amplitudes, integrals)


def solution(mesh):
    in_specs = (P(None, None, ("rep", "wide"), None), P(None, "rep", "wide"), P())
    out_specs = P(None, ("rep", "wide"), None)
    return jax.shard_map(
        functools.partial(per_device, mesh.shape["rep"], mesh.shape["wide"]),
        mesh=mesh, in_specs=in_specs, out_specs=out_specs, check_vma=False,
    )
```

```python
import functools

import jax
import jax.numpy as jnp
from jax import lax
from jax.experimental import pallas as pl
from jax.experimental.pallas import tpu as pltpu
from jax.sharding import PartitionSpec as P

MESH = pl.DeviceIdType.MESH
MIB = 2**20
GROUP = 8


def ladder_kernel(reps, members, live, amp, integ, out, rows, relay, cols, part, landed, summed, placed, direct,
                  b_send, b_recv, b_own, a_send, a_recv, y_send, y_recv, p_send, p_recv,
                  r_send, r_recv, l_send, l_recv, o_send, o_recv, d_send, d_recv):
    r, w = lax.axis_index("rep"), lax.axis_index("wide")
    up, down, across = (r + 1) % reps, (r + reps - 1) % reps, (r + 2) % reps
    groups = members // GROUP
    plane, seat = w // GROUP, w % GROUP
    cuts = integ.shape[1]
    owned, depth = amp.shape[2], amp.shape[3]
    halves = amp.shape[0] // reps
    beside = {1: (down, up), 2: (across, across), 3: (up, down)}

    def irrep(behind, half):
        return (r + reps - behind) % reps + reps * half

    def remote(src, dst, send, recv, rep, member):
        return pltpu.make_async_remote_copy(
            src_ref=src, dst_ref=dst, send_sem=send, recv_sem=recv, device_id=(rep, member), device_id_type=MESH
        )

    def wait_for(ref, sem):
        pltpu.make_async_copy(ref, ref, sem).wait()

    def other(t):
        return (w + t) % members

    def neighbour(t):
        return plane * GROUP + (seat + t) % GROUP

    barrier = pltpu.get_barrier_semaphore()

    def greet(rep, member):
        pl.semaphore_signal(barrier, inc=1, device_id=(rep, member), device_id_type=MESH)

    def greet_rep(t, carry):
        greet(r, other(t))
        return carry

    def greet_group(t, carry):
        greet(up, neighbour(t))
        greet(down, neighbour(t))
        return carry

    greet(across, w)
    lax.fori_loop(0, GROUP, greet_group, 0)
    lax.fori_loop(1, members, greet_rep, 0)
    pl.semaphore_wait(barrier, members + 2 * GROUP)

    mine, theirs = pl.ds(0, cuts), pl.ds(cuts, cuts)

    def send_columns(half):
        remote(integ.at[irrep(3, half)], cols.at[half, 0, theirs], b_send.at[half, 0], b_recv.at[half, 0], up, w).start()
        remote(integ.at[irrep(2, half)], cols.at[half, 1, theirs], b_send.at[half, 1], b_recv.at[half, 1], down, w).start()

    def own_columns(half, role):
        return pltpu.make_async_copy(integ.at[irrep(role, half)], cols.at[half, role, mine], b_own.at[half, role])

    def columns_ready(half):
        for role in range(2):
            own_columns(half, role).wait()
            wait_for(cols.at[half, role, theirs], b_recv.at[half, role])

    def arriving(behind, half):
        return rows.at[half, behind, 0] if behind < 2 else relay.at[half, behind - 2]

    def spread(behind, half):
        g, target = irrep(behind, half), arriving(behind, half)
        send, recv = a_send.at[half, behind], a_recv.at[half, behind]
        pltpu.make_async_copy(amp.at[g, w], target.at[w], recv).start()

        def one(t, carry):
            remote(amp.at[g, other(t)], target.at[w], send, recv, r, other(t)).start()
            return carry

        lax.fori_loop(1, members, one, 0)

    def arrived(behind, half):
        wait_for(arriving(behind, half), a_recv.at[half, behind])

    def along(src, half, role, slot, rep):
        return remote(src, rows.at[half, role, slot], y_send.at[half, role, slot - 1], y_recv.at[half, role, slot - 1],
                      rep, w)

    def relay_rows(half):
        arrived(3, half)
        along(relay.at[half, 1], half, 0, 1, up).start()
        arrived(2, half)
        along(relay.at[half, 0], half, 1, 1, down).start()

    def forward_rows(half):
        took(half, 0, 1)
        along(rows.at[half, 0, 1], half, 1, 2, up).start()
        took(half, 1, 1)
        along(rows.at[half, 1, 1], half, 0, 2, down).start()

    def exchange_rows(half):
        arrived(0, half)
        along(rows.at[half, 0, 0], half, 1, 3, up).start()
        arrived(1, half)
        along(rows.at[half, 1, 0], half, 0, 3, down).start()

    def took(half, role, slot):
        wait_for(rows.at[half, role, slot], y_recv.at[half, role, slot - 1])

    def group_at(step):
        return pl.ds((plane + step) % groups * GROUP, GROUP)

    def exchange_piece(step):
        for role, rep in ((0, up), (1, down)):
            remote(rows.at[1, role, 0, group_at(step)], rows.at[1, 1 - role, 3, group_at(step)],
                   p_send.at[role, step], p_recv.at[1 - role, step], rep, w).start()

    def product(left, half, role):
        return lax.dot_general(left, cols[half, role], (((1,), (1,)), ((), ())), preferred_element_type=jnp.float32)

    def multiply(half, role, slot):
        left = rows[half, role, slot].reshape(members * owned, depth)
        part[half, role, :, slot] = product(left, half, role).reshape(members, owned, 2 * cuts)

    def multiply_piece(step):
        for role in range(2):
            at = group_at(step)
            wait_for(rows.at[1, role, 3, at], p_recv.at[role, step])
            left = rows[1, role, 3, at].reshape(GROUP * owned, depth)
            part[1, role, at, 3] = product(left, 1, role).reshape(GROUP, owned, 2 * cuts)

    stages = (pl.ds(0, 2), pl.ds(2, 1), pl.ds(3, 1))

    def give(half, stage):
        slots, send, recv = stages[stage], r_send.at[half, stage], r_recv.at[half, stage]
        pltpu.make_async_copy(part.at[half, :, w, slots], landed.at[half, :, w, slots], recv).start()

        def one(t, carry):
            remote(
                part.at[half, :, other(t), slots], landed.at[half, :, w, slots], send, recv, r, other(t)
            ).start()
            return carry

        lax.fori_loop(1, members, one, 0)

    def give_piece(step):
        base = (plane + step) % groups * GROUP

        def one(t, carry):
            member = base + (seat + t) % GROUP
            remote(part.at[1, :, member, 3], landed.at[1, :, step * GROUP + seat, 3], l_send, l_recv, r, member).start()
            return carry

        lax.fori_loop(0, GROUP, one, 0)

    def give_direct():
        def one(t, carry):
            for role in range(2):
                remote(part.at[1, role, neighbour(t), 3], direct.at[role, seat], d_send, d_recv,
                       beside[3][role], neighbour(t)).start()
            return carry

        lax.fori_loop(0, GROUP, one, 0)

    def add_up(half, stage):
        slots = stages[stage]
        wait_for(landed.at[half, :, :, slots], r_recv.at[half, stage])
        summed[half, :, slots] = jnp.sum(landed[half, :, :, slots], axis=1)
        hand_out(half, ((0, 1), (2,), (3,))[stage])

    far = pl.ds(GROUP, members - GROUP)

    def add_up_pieces():
        wait_for(landed.at[1, :, far, 3], l_recv)
        summed[1, :, 3] = jnp.sum(landed[1, :, far, 3], axis=1)
        hand_out(1, (3,))

    def hand_out(half, slots):
        for role in range(2):
            g = irrep(role, half)
            for slot in slots:
                if slot == 0:
                    placed[g, role] = summed[half, role, 0]
                else:
                    remote(summed.at[half, role, slot], placed.at[g, role], o_send.at[half, role, slot - 1],
                           o_recv.at[half], beside[slot][role], w).start()

    def finish(half):
        index = (r * members + w) * owned + lax.broadcasted_iota(jnp.int32, (owned, reps * cuts), 0)
        for p in range(reps):
            g = reps * half + p
            found = {}
            for role, beyond in ((0, reps - 1), (1, 1)):
                here = (p + role) % reps
                found[here] = placed[g, role, :, :cuts]
                found[(here + beyond) % reps] = placed[g, role, :, cuts:]
            ladder = jnp.concatenate([found[q] for q in range(reps)], axis=1)
            out[g] = jnp.where(index < live[g], ladder, 0.0).astype(out.dtype)

    send_columns(0)
    spread(3, 0)
    spread(2, 0)
    for half in range(halves):
        for role in range(2):
            own_columns(half, role).start()
    spread(3, 1)
    spread(2, 1)
    relay_rows(0)
    send_columns(1)
    spread(0, 0)
    spread(1, 0)
    relay_rows(1)
    spread(0, 1)
    spread(1, 1)
    forward_rows(0)
    exchange_rows(0)

    columns_ready(0)
    for role in range(2):
        multiply(0, role, 0)
        multiply(0, role, 1)
    give(0, 0)
    forward_rows(1)
    arrived(0, 1)
    arrived(1, 1)
    for step in (1, 2, 3, 0):
        exchange_piece(step)
    add_up(0, 0)
    columns_ready(1)
    for role in range(2):
        multiply(1, role, 0)
        multiply(1, role, 1)
    give(1, 0)
    for role in range(2):
        took(0, role, 2)
        multiply(0, role, 2)
    give(0, 1)
    add_up(1, 0)
    for role in range(2):
        took(0, role, 3)
        multiply(0, role, 3)
    give(0, 2)
    add_up(0, 1)
    for role in range(2):
        took(1, role, 2)
        multiply(1, role, 2)
    give(1, 1)
    add_up(0, 2)
    multiply_piece(1)
    give_piece(1)
    add_up(1, 1)
    multiply_piece(2)
    give_piece(2)
    wait_for(placed.at[pl.ds(0, reps - 1)], o_recv.at[0])
    finish(0)
    multiply_piece(3)
    give_piece(3)
    multiply_piece(0)
    give_direct()
    add_up_pieces()
    wait_for(direct, d_recv)
    wait_for(placed.at[pl.ds(reps, reps - 1)], o_recv.at[1])
    for role, behind in ((0, 1), (1, 0)):
        g = irrep(behind, 1)
        placed[g, role] = placed[g, role] + jnp.sum(direct[role], axis=0)
    finish(1)

    some = pl.ds(1, members - 1)
    for half in range(halves):
        for role in range(2):
            wait_for(cols.at[half, role, theirs], b_send.at[half, role])
            for slot in range(3):
                wait_for(summed.at[half, role, slot], o_send.at[half, role, slot])
                if (half, slot) != (1, 2):
                    wait_for(rows.at[half, role, slot], y_send.at[half, role, slot])
        for behind in range(reps):
            wait_for(relay.at[half, 0, some], a_send.at[half, behind])
        for stage in range(3 - half):
            wait_for(landed.at[half, :, some, stages[stage]], r_send.at[half, stage])
    for role in range(2):
        for step in range(groups):
            wait_for(rows.at[1, role, 0, group_at(step)], p_send.at[role, step])
    wait_for(landed.at[1, :, far, 3], l_send)
    wait_for(direct, d_send)


def per_device(reps, members, amplitudes, integrals, live_pairs):
    irreps, blocks, owned, depth = amplitudes.shape
    cuts = integrals.shape[1]
    halves = irreps // reps
    dma = pltpu.SemaphoreType.DMA
    f32, bf16 = jnp.float32, jnp.bfloat16
    return pl.pallas_call(
        functools.partial(ladder_kernel, reps, members),
        out_shape=jax.ShapeDtypeStruct((irreps, owned, reps * cuts), bf16),
        in_specs=[pl.BlockSpec(memory_space=pltpu.SMEM)] + [pl.BlockSpec(memory_space=pl.ANY)] * 2,
        out_specs=pl.BlockSpec(memory_space=pltpu.VMEM),
        scratch_shapes=[
            pltpu.VMEM((halves, 2, 4, members, owned, depth), bf16),
            pltpu.VMEM((halves, 2, members, owned, depth), bf16),
            pltpu.VMEM((halves, 2, 2 * cuts, depth), bf16),
            pltpu.VMEM((halves, 2, members, 4, owned, 2 * cuts), f32),
            pltpu.VMEM((halves, 2, members, 4, owned, 2 * cuts), f32),
            pltpu.VMEM((halves, 2, 4, owned, 2 * cuts), f32),
            pltpu.VMEM((irreps, 2, owned, 2 * cuts), f32),
            pltpu.VMEM((2, GROUP, owned, 2 * cuts), f32),
            dma((halves, 2)), dma((halves, 2)), dma((halves, 2)),
            dma((halves, 4)), dma((halves, 4)),
            dma((halves, 2, 3)), dma((halves, 2, 3)),
            dma((2, 4)), dma((2, 4)),
            dma((halves, 3)), dma((halves, 3)),
            dma, dma,
            dma((halves, 2, 3)), dma((halves,)),
            dma, dma,
        ],
        compiler_params=pltpu.CompilerParams(collective_id=0, has_side_effects=True, vmem_limit_bytes=52 * MIB),
        cost_estimate=pl.CostEstimate(
            flops=2 * irreps * owned * members * 4 * cuts * depth, bytes_accessed=26 * MIB, transcendentals=0
        ),
        name="ladder",
    )(live_pairs, amplitudes, integrals)


def solution(mesh):
    in_specs = (P(None, None, ("rep", "wide"), None), P(None, "rep", "wide"), P())
    out_specs = P(None, ("rep", "wide"), None)
    return jax.shard_map(
        functools.partial(per_device, mesh.shape["rep"], mesh.shape["wide"]),
        mesh=mesh, in_specs=in_specs, out_specs=out_specs, check_vma=False,
    )
```

```python
import functools

import jax
import jax.numpy as jnp
from jax import lax
from jax.experimental import pallas as pl
from jax.experimental.pallas import tpu as pltpu
from jax.sharding import PartitionSpec as P

MESH = pl.DeviceIdType.MESH
MIB = 2**20
GROUP = 8


def ladder_kernel(reps, members, live, amp, integ, out, rows, relay, cols, part, landed, summed, placed, direct,
                  b_send, b_recv, b_own, a_send, a_recv, y_send, y_recv, p_send, p_recv,
                  r_send, r_recv, l_send, l_recv, o_send, o_recv, d_send, d_recv, counts, c_got):
    r, w = lax.axis_index("rep"), lax.axis_index("wide")
    up, down, across = (r + 1) % reps, (r + reps - 1) % reps, (r + 2) % reps
    groups = members // GROUP
    plane, seat = w // GROUP, w % GROUP
    cuts = integ.shape[1]
    owned, depth = amp.shape[2], amp.shape[3]
    halves = amp.shape[0] // reps
    beside = {1: (down, up), 2: (across, across), 3: (up, down)}

    def irrep(behind, half):
        return (r + reps - behind) % reps + reps * half

    def remote(src, dst, send, recv, rep, member):
        return pltpu.make_async_remote_copy(
            src_ref=src, dst_ref=dst, send_sem=send, recv_sem=recv, device_id=(rep, member), device_id_type=MESH
        )

    def wait_for(ref, sem):
        pltpu.make_async_copy(ref, ref, sem).wait()

    def other(t):
        return (w + t) % members

    def neighbour(t):
        return plane * GROUP + (seat + t) % GROUP

    fetch = pltpu.make_async_copy(live, counts, c_got)
    fetch.start()
    barrier = pltpu.get_barrier_semaphore()

    def greet(rep, member):
        pl.semaphore_signal(barrier, inc=1, device_id=(rep, member), device_id_type=MESH)

    def greet_rep(t, carry):
        greet(r, other(t))
        return carry

    def greet_group(t, carry):
        greet(up, neighbour(t))
        greet(down, neighbour(t))
        return carry

    greet(across, w)
    lax.fori_loop(0, GROUP, greet_group, 0)
    lax.fori_loop(1, members, greet_rep, 0)
    pl.semaphore_wait(barrier, members + 2 * GROUP)

    mine, theirs = pl.ds(0, cuts), pl.ds(cuts, cuts)
    near, far = pl.ds(0, GROUP), pl.ds(GROUP, members - GROUP)
    far_steps = ((1, 2), (3,))
    far_pieces = (pl.ds(GROUP, 2 * GROUP), pl.ds(3 * GROUP, GROUP))
    stretches = (pl.ds(0, depth // 2), pl.ds(depth // 2, depth // 2))

    def send_columns(half):
        remote(integ.at[irrep(3, half)], cols.at[half, 0, theirs], b_send.at[half, 0], b_recv.at[half, 0], up, w).start()
        remote(integ.at[irrep(2, half)], cols.at[half, 1, theirs], b_send.at[half, 1], b_recv.at[half, 1], down, w).start()

    def own_columns(half, role):
        return pltpu.make_async_copy(integ.at[irrep(role, half)], cols.at[half, role, mine], b_own.at[half, role])

    def columns_ready(half):
        for role in range(2):
            own_columns(half, role).wait()
            wait_for(cols.at[half, role, theirs], b_recv.at[half, role])

    def arriving(behind, half):
        return rows.at[half, behind, 0] if behind < 2 else relay.at[half, behind - 2]

    def spread(behind, half):
        g, target = irrep(behind, half), arriving(behind, half)
        send, recv = a_send.at[half, behind], a_recv.at[half, behind]
        pltpu.make_async_copy(amp.at[g, w], target.at[w], recv).start()

        def one(t, carry):
            remote(amp.at[g, other(t)], target.at[w], send, recv, r, other(t)).start()
            return carry

        lax.fori_loop(1, members, one, 0)

    def arrived(behind, half):
        wait_for(arriving(behind, half), a_recv.at[half, behind])

    def along(src, half, role, slot, rep):
        return remote(src, rows.at[half, role, slot], y_send.at[half, role, slot - 1], y_recv.at[half, role, slot - 1],
                      rep, w)

    def relay_rows(half):
        arrived(3, half)
        along(relay.at[half, 1], half, 0, 1, up).start()
        arrived(2, half)
        along(relay.at[half, 0], half, 1, 1, down).start()

    def forward_rows(half):
        took(half, 0, 1)
        along(rows.at[half, 0, 1], half, 1, 2, up).start()
        took(half, 1, 1)
        along(rows.at[half, 1, 1], half, 0, 2, down).start()

    def exchange_rows(half):
        arrived(0, half)
        along(rows.at[half, 0, 0], half, 1, 3, up).start()
        arrived(1, half)
        along(rows.at[half, 1, 0], half, 0, 3, down).start()

    def took(half, role, slot):
        wait_for(rows.at[half, role, slot], y_recv.at[half, role, slot - 1])

    def group_at(step):
        return pl.ds((plane + step) % groups * GROUP, GROUP)

    def exchange_far(piece):
        for role, rep in ((0, up), (1, down)):
            for step in far_steps[piece]:
                remote(rows.at[1, role, 0, group_at(step)], rows.at[1, 1 - role, 3, pl.ds(step * GROUP, GROUP)],
                       p_send.at[role, piece], p_recv.at[1 - role, piece], rep, w).start()

    def exchange_near(stretch):
        for role, rep in ((0, up), (1, down)):
            remote(rows.at[1, role, 0, group_at(0), :, stretches[stretch]], rows.at[1, 1 - role, 3, near, :, stretches[stretch]],
                   p_send.at[role, 2 + stretch], p_recv.at[1 - role, 2 + stretch], rep, w).start()

    def product(left, half, role):
        return lax.dot_general(left, cols[half, role], (((1,), (1,)), ((), ())), preferred_element_type=jnp.float32)

    def multiply(half, role, slot):
        left = rows[half, role, slot].reshape(members * owned, depth)
        part[half, role, :, slot] = product(left, half, role).reshape(members, owned, 2 * cuts)

    def multiply_far(piece):
        at = far_pieces[piece]
        for role in range(2):
            wait_for(rows.at[1, role, 3, at], p_recv.at[role, piece])
            left = rows[1, role, 3, at].reshape(at.size * owned, depth)
            part[1, role, at, 3] = product(left, 1, role).reshape(at.size, owned, 2 * cuts)

    def multiply_near(role, stretch):
        inner = stretches[stretch]
        wait_for(rows.at[1, role, 3, near, :, inner], p_recv.at[role, 2 + stretch])
        left = rows[1, role, 3, near, :, inner].reshape(GROUP * owned, depth // 2)
        some = lax.dot_general(
            left, cols[1, role, :, inner], (((1,), (1,)), ((), ())), preferred_element_type=jnp.float32
        ).reshape(GROUP, owned, 2 * cuts)
        part[1, role, near, 3] = some if stretch == 0 else part[1, role, near, 3] + some

    stages = (pl.ds(0, 2), pl.ds(2, 1), pl.ds(3, 1))

    def give(half, stage):
        slots, send, recv = stages[stage], r_send.at[half, stage], r_recv.at[half, stage]
        pltpu.make_async_copy(part.at[half, :, w, slots], landed.at[half, :, w, slots], recv).start()

        def one(t, carry):
            remote(
                part.at[half, :, other(t), slots], landed.at[half, :, w, slots], send, recv, r, other(t)
            ).start()
            return carry

        lax.fori_loop(1, members, one, 0)

    def give_far(piece):
        def one(t, carry):
            step, place = t // GROUP, (seat + t) % GROUP
            member = (plane + step) % groups * GROUP + place
            remote(part.at[1, :, step * GROUP + place, 3], landed.at[1, :, step * GROUP + seat, 3], l_send, l_recv,
                   r, member).start()
            return carry

        at = far_pieces[piece]
        lax.fori_loop(at.start, at.start + at.size, one, 0)

    def give_near(role):
        def one(t, carry):
            remote(part.at[1, role, (seat + t) % GROUP, 3], direct.at[role, seat], d_send.at[role], d_recv.at[role],
                   beside[3][role], neighbour(t)).start()
            return carry

        lax.fori_loop(0, GROUP, one, 0)

    def add_up(half, stage):
        slots = stages[stage]
        wait_for(landed.at[half, :, :, slots], r_recv.at[half, stage])
        summed[half, :, slots] = jnp.sum(landed[half, :, :, slots], axis=1)
        hand_out(half, ((0, 1), (2,), (3,))[stage])

    def add_up_far():
        wait_for(landed.at[1, :, far, 3], l_recv)
        summed[1, :, 3] = jnp.sum(landed[1, :, far, 3], axis=1)
        hand_out(1, (3,))

    def hand_out(half, slots):
        for role in range(2):
            g = irrep(role, half)
            for slot in slots:
                if slot == 0:
                    placed[g, role] = summed[half, role, 0]
                else:
                    remote(summed.at[half, role, slot], placed.at[g, role], o_send.at[half, role, slot - 1],
                           o_recv.at[half], beside[slot][role], w).start()

    def finish(half):
        index = (r * members + w) * owned + lax.broadcasted_iota(jnp.int32, (owned, reps * cuts), 0)
        for p in range(reps):
            g = reps * half + p
            found = {}
            for role, beyond in ((0, reps - 1), (1, 1)):
                here = (p + role) % reps
                found[here] = placed[g, role, :, :cuts]
                found[(here + beyond) % reps] = placed[g, role, :, cuts:]
            ladder = jnp.concatenate([found[q] for q in range(reps)], axis=1)
            out[g] = jnp.where(index < counts[g], ladder, 0.0).astype(out.dtype)

    send_columns(0)
    spread(3, 0)
    spread(2, 0)
    for half in range(halves):
        for role in range(2):
            own_columns(half, role).start()
    spread(3, 1)
    spread(2, 1)
    relay_rows(0)
    send_columns(1)
    spread(0, 0)
    spread(1, 0)
    relay_rows(1)
    spread(0, 1)
    spread(1, 1)
    forward_rows(0)
    exchange_rows(0)

    columns_ready(0)
    for role in range(2):
        multiply(0, role, 0)
        multiply(0, role, 1)
    give(0, 0)
    forward_rows(1)
    arrived(0, 1)
    arrived(1, 1)
    add_up(0, 0)
    columns_ready(1)
    for role in range(2):
        multiply(1, role, 0)
        multiply(1, role, 1)
    give(1, 0)
    for role in range(2):
        took(0, role, 2)
        multiply(0, role, 2)
    give(0, 1)
    add_up(1, 0)
    for role in range(2):
        took(0, role, 3)
        multiply(0, role, 3)
    give(0, 2)
    add_up(0, 1)
    exchange_far(0)
    for role in range(2):
        took(1, role, 2)
        multiply(1, role, 2)
    give(1, 1)
    add_up(0, 2)
    exchange_far(1)
    exchange_near(0)
    exchange_near(1)
    some = pl.ds(1, members - 1)
    for half in range(halves):
        for role in range(2):
            wait_for(cols.at[half, role, theirs], b_send.at[half, role])
            wait_for(rows.at[half, role, 0], y_send.at[half, role, 0])
        for behind in range(reps):
            wait_for(relay.at[half, 0, some], a_send.at[half, behind])
        wait_for(landed.at[half, :, some, stages[0]], r_send.at[half, 0])
    for stage in (1, 2):
        wait_for(landed.at[0, :, some, stages[stage]], r_send.at[0, stage])
        for role in range(2):
            wait_for(rows.at[0, role, 0], y_send.at[0, role, stage])
    multiply_far(0)
    give_far(0)
    add_up(1, 1)
    fetch.wait()
    wait_for(placed.at[pl.ds(0, reps - 1)], o_recv.at[0])
    finish(0)
    multiply_far(1)
    give_far(1)
    for role in range(2):
        multiply_near(role, 0)
    for role in range(2):
        multiply_near(role, 1)
        give_near(role)
    add_up_far()
    for role in range(2):
        wait_for(rows.at[1, role, 0], y_send.at[1, role, 1])
        for index in range(2):
            wait_for(rows.at[1, role, 0, far_pieces[index]], p_send.at[role, index])
            wait_for(rows.at[1, role, 0, near, :, stretches[index]], p_send.at[role, 2 + index])
        for slot in range(3):
            wait_for(summed.at[0, role, slot], o_send.at[0, role, slot])
        for slot in range(2):
            wait_for(summed.at[1, role, slot], o_send.at[1, role, slot])
    wait_for(landed.at[1, :, some, stages[1]], r_send.at[1, 1])
    wait_for(landed.at[1, :, far, 3], l_send)
    for role in range(2):
        wait_for(direct.at[role], d_send.at[role])
        wait_for(direct.at[role], d_recv.at[role])
        wait_for(summed.at[1, role, 2], o_send.at[1, role, 2])
    wait_for(placed.at[pl.ds(reps, reps - 1)], o_recv.at[1])
    for role, behind in ((0, 1), (1, 0)):
        g = irrep(behind, 1)
        placed[g, role] = placed[g, role] + jnp.sum(direct[role], axis=0)
    finish(1)


def per_device(reps, members, amplitudes, integrals, live_pairs):
    irreps, blocks, owned, depth = amplitudes.shape
    cuts = integrals.shape[1]
    halves = irreps // reps
    dma = pltpu.SemaphoreType.DMA
    f32, bf16 = jnp.float32, jnp.bfloat16
    return pl.pallas_call(
        functools.partial(ladder_kernel, reps, members),
        out_shape=jax.ShapeDtypeStruct((irreps, owned, reps * cuts), bf16),
        in_specs=[pl.BlockSpec(memory_space=pl.ANY)] * 3,
        out_specs=pl.BlockSpec(memory_space=pltpu.VMEM),
        scratch_shapes=[
            pltpu.VMEM((halves, 2, 4, members, owned, depth), bf16),
            pltpu.VMEM((halves, 2, members, owned, depth), bf16),
            pltpu.VMEM((halves, 2, 2 * cuts, depth), bf16),
            pltpu.VMEM((halves, 2, members, 4, owned, 2 * cuts), f32),
            pltpu.VMEM((halves, 2, members, 4, owned, 2 * cuts), f32),
            pltpu.VMEM((halves, 2, 4, owned, 2 * cuts), f32),
            pltpu.VMEM((irreps, 2, owned, 2 * cuts), f32),
            pltpu.VMEM((2, GROUP, owned, 2 * cuts), f32),
            dma((halves, 2)), dma((halves, 2)), dma((halves, 2)),
            dma((halves, 4)), dma((halves, 4)),
            dma((halves, 2, 3)), dma((halves, 2, 3)),
            dma((2, 4)), dma((2, 4)),
            dma((halves, 3)), dma((halves, 3)),
            dma, dma,
            dma((halves, 2, 3)), dma((halves,)),
            dma((2,)), dma((2,)),
            pltpu.SMEM((irreps,), jnp.int32), dma,
        ],
        compiler_params=pltpu.CompilerParams(collective_id=0, has_side_effects=True, vmem_limit_bytes=52 * MIB),
        cost_estimate=pl.CostEstimate(
            flops=2 * irreps * owned * members * 4 * cuts * depth, bytes_accessed=26 * MIB, transcendentals=0
        ),
        name="ladder",
    )(live_pairs, amplitudes, integrals)


def solution(mesh):
    in_specs = (P(None, None, ("rep", "wide"), None), P(None, "rep", "wide"), P())
    out_specs = P(None, ("rep", "wide"), None)
    return jax.shard_map(
        functools.partial(per_device, mesh.shape["rep"], mesh.shape["wide"]),
        mesh=mesh, in_specs=in_specs, out_specs=out_specs, check_vma=False,
    )
```

```python
import functools

import jax
import jax.numpy as jnp
from jax import lax
from jax.experimental import pallas as pl
from jax.experimental.pallas import tpu as pltpu
from jax.sharding import PartitionSpec as P

MESH = pl.DeviceIdType.MESH
MIB = 2**20
GROUP = 8


def ladder_kernel(reps, members, amp, integ, out, rows, relay, cols, part, landed, summed, placed, direct,
                  b_send, b_recv, b_own, a_send, a_recv, y_send, y_recv, p_send, p_recv,
                  r_send, r_recv, l_send, l_recv, o_send, o_recv, d_send, d_recv):
    r, w = lax.axis_index("rep"), lax.axis_index("wide")
    up, down, across = (r + 1) % reps, (r + reps - 1) % reps, (r + 2) % reps
    groups = members // GROUP
    plane, seat = w // GROUP, w % GROUP
    cuts = integ.shape[1]
    owned, depth = amp.shape[2], amp.shape[3]
    halves = amp.shape[0] // reps
    beside = {1: (down, up), 2: (across, across), 3: (up, down)}

    def irrep(behind, half):
        return (r + reps - behind) % reps + reps * half

    def remote(src, dst, send, recv, rep, member):
        return pltpu.make_async_remote_copy(
            src_ref=src, dst_ref=dst, send_sem=send, recv_sem=recv, device_id=(rep, member), device_id_type=MESH
        )

    def wait_for(ref, sem):
        pltpu.make_async_copy(ref, ref, sem).wait()

    def other(t):
        return (w + t) % members

    barrier = pltpu.get_barrier_semaphore()

    def greet(rep, member):
        pl.semaphore_signal(barrier, inc=1, device_id=(rep, member), device_id_type=MESH)

    def greet_rep(t, carry):
        greet(r, other(t))
        return carry

    greet(up, w)
    greet(down, w)
    lax.fori_loop(1, members, greet_rep, 0)
    pl.semaphore_wait(barrier, members + 1)

    mine, theirs = pl.ds(0, cuts), pl.ds(cuts, cuts)
    near = pl.ds(0, GROUP)
    far_steps = ((1, 2), (3,))
    far_pieces = (pl.ds(GROUP, 2 * GROUP), pl.ds(3 * GROUP, GROUP))
    stretches = (pl.ds(0, depth // 2), pl.ds(depth // 2, depth // 2))

    def send_columns(half):
        remote(integ.at[irrep(3, half)], cols.at[half, 0, theirs], b_send.at[half, 0], b_recv.at[half, 0], up, w).start()
        remote(integ.at[irrep(2, half)], cols.at[half, 1, theirs], b_send.at[half, 1], b_recv.at[half, 1], down, w).start()

    def own_columns(half, role):
        return pltpu.make_async_copy(integ.at[irrep(role, half)], cols.at[half, role, mine], b_own.at[half, role])

    def columns_ready(half):
        for role in range(2):
            own_columns(half, role).wait()
            wait_for(cols.at[half, role, theirs], b_recv.at[half, role])

    def arriving(behind, half):
        return rows.at[half, behind, 0] if behind < 2 else relay.at[half, behind - 2]

    def spread(behind, half):
        g, target = irrep(behind, half), arriving(behind, half)
        send, recv = a_send.at[half, behind], a_recv.at[half, behind]
        pltpu.make_async_copy(amp.at[g, w], target.at[w], recv).start()

        def one(t, carry):
            remote(amp.at[g, other(t)], target.at[w], send, recv, r, other(t)).start()
            return carry

        lax.fori_loop(1, members, one, 0)

    def arrived(behind, half):
        wait_for(arriving(behind, half), a_recv.at[half, behind])

    def along(src, half, role, slot, rep):
        return remote(src, rows.at[half, role, slot], y_send.at[half, role, slot - 1], y_recv.at[half, role, slot - 1],
                      rep, w)

    def relay_rows(half):
        arrived(3, half)
        along(relay.at[half, 1], half, 0, 1, up).start()
        arrived(2, half)
        along(relay.at[half, 0], half, 1, 1, down).start()

    def forward_rows(half):
        took(half, 0, 1)
        along(rows.at[half, 0, 1], half, 1, 2, up).start()
        took(half, 1, 1)
        along(rows.at[half, 1, 1], half, 0, 2, down).start()

    def exchange_rows(half):
        arrived(0, half)
        along(rows.at[half, 0, 0], half, 1, 3, up).start()
        arrived(1, half)
        along(rows.at[half, 1, 0], half, 0, 3, down).start()

    def took(half, role, slot):
        wait_for(rows.at[half, role, slot], y_recv.at[half, role, slot - 1])

    def group_at(step):
        return pl.ds((plane + step) % groups * GROUP, GROUP)

    def exchange_far(piece):
        for role, rep in ((0, up), (1, down)):
            for step in far_steps[piece]:
                remote(rows.at[1, role, 0, group_at(step)], rows.at[1, 1 - role, 3, pl.ds(step * GROUP, GROUP)],
                       p_send.at[role, piece], p_recv.at[1 - role, piece], rep, w).start()

    def exchange_near(stretch):
        for role, rep in ((0, up), (1, down)):
            remote(rows.at[1, role, 0, group_at(0), :, stretches[stretch]], rows.at[1, 1 - role, 3, near, :, stretches[stretch]],
                   p_send.at[role, 2 + stretch], p_recv.at[1 - role, 2 + stretch], rep, w).start()

    def product(left, half, role):
        return lax.dot_general(left, cols[half, role], (((1,), (1,)), ((), ())), preferred_element_type=jnp.float32)

    def multiply(half, role, slot):
        left = rows[half, role, slot].reshape(members * owned, depth)
        part[half, role, :, slot] = product(left, half, role).reshape(members, owned, 2 * cuts)

    def multiply_far(piece):
        at = far_pieces[piece]
        for role in range(2):
            wait_for(rows.at[1, role, 3, at], p_recv.at[role, piece])
            left = rows[1, role, 3, at].reshape(at.size * owned, depth)
            part[1, role, at, 3] = product(left, 1, role).reshape(at.size, owned, 2 * cuts)

    def multiply_near(role, stretch):
        inner = stretches[stretch]
        wait_for(rows.at[1, role, 3, near, :, inner], p_recv.at[role, 2 + stretch])
        left = rows[1, role, 3, near, :, inner].reshape(GROUP * owned, depth // 2)
        some = lax.dot_general(
            left, cols[1, role, :, inner], (((1,), (1,)), ((), ())), preferred_element_type=jnp.float32
        ).reshape(GROUP, owned, 2 * cuts)
        part[1, role, near, 3] = some if stretch == 0 else part[1, role, near, 3] + some

    stages = (pl.ds(0, 2), pl.ds(2, 1), pl.ds(3, 1))

    def give(half, stage):
        slots, send, recv = stages[stage], r_send.at[half, stage], r_recv.at[half, stage]
        pltpu.make_async_copy(part.at[half, :, w, slots], landed.at[half, :, w, slots], recv).start()

        def one(t, carry):
            remote(
                part.at[half, :, other(t), slots], landed.at[half, :, w, slots], send, recv, r, other(t)
            ).start()
            return carry

        lax.fori_loop(1, members, one, 0)

    def give_far():
        def one(t, carry):
            step, place = t // GROUP, (seat + t) % GROUP
            member = (plane + step) % groups * GROUP + place
            remote(part.at[1, :, step * GROUP + place, 3], landed.at[1, :, step * GROUP + seat, 3], l_send, l_recv,
                   r, member).start()
            return carry

        at = far_pieces[0]
        lax.fori_loop(at.start, at.start + at.size, one, 0)

    def give_direct(role, step, kept):
        def one(t, carry):
            place = (seat + t) % GROUP
            remote(part.at[1, role, step * GROUP + place, 3], direct.at[role, kept, seat], d_send.at[role],
                   d_recv.at[role], beside[3][role], (plane + step) % groups * GROUP + place).start()
            return carry

        lax.fori_loop(0, GROUP, one, 0)

    def add_up(half, stage):
        slots = stages[stage]
        wait_for(landed.at[half, :, :, slots], r_recv.at[half, stage])
        summed[half, :, slots] = jnp.sum(landed[half, :, :, slots], axis=1)
        hand_out(half, ((0, 1), (2,), (3,))[stage])

    def add_up_far():
        wait_for(landed.at[1, :, far_pieces[0], 3], l_recv)
        summed[1, :, 3] = jnp.sum(landed[1, :, far_pieces[0], 3], axis=1)
        hand_out(1, (3,))

    def hand_out(half, slots):
        for role in range(2):
            g = irrep(role, half)
            for slot in slots:
                if slot == 0:
                    placed[g, role] = summed[half, role, 0]
                else:
                    remote(summed.at[half, role, slot], placed.at[g, role], o_send.at[half, role, slot - 1],
                           o_recv.at[half], beside[slot][role], w).start()

    def finish(half):
        for p in range(reps):
            g = reps * half + p
            found = {}
            for role, beyond in ((0, reps - 1), (1, 1)):
                here = (p + role) % reps
                found[here] = placed[g, role, :, :cuts]
                found[(here + beyond) % reps] = placed[g, role, :, cuts:]
            out[g] = jnp.concatenate([found[q] for q in range(reps)], axis=1).astype(out.dtype)

    send_columns(0)
    spread(3, 0)
    spread(2, 0)
    for half in range(halves):
        for role in range(2):
            own_columns(half, role).start()
    spread(3, 1)
    spread(2, 1)
    relay_rows(0)
    send_columns(1)
    spread(0, 0)
    spread(1, 0)
    relay_rows(1)
    spread(0, 1)
    spread(1, 1)
    forward_rows(0)
    exchange_rows(0)

    columns_ready(0)
    for role in range(2):
        multiply(0, role, 0)
        multiply(0, role, 1)
    give(0, 0)
    forward_rows(1)
    arrived(0, 1)
    arrived(1, 1)
    add_up(0, 0)
    columns_ready(1)
    for role in range(2):
        multiply(1, role, 0)
        multiply(1, role, 1)
    give(1, 0)
    for role in range(2):
        took(0, role, 2)
        multiply(0, role, 2)
    give(0, 1)
    add_up(1, 0)
    for role in range(2):
        took(0, role, 3)
        multiply(0, role, 3)
    give(0, 2)
    add_up(0, 1)
    exchange_far(0)
    for role in range(2):
        took(1, role, 2)
        multiply(1, role, 2)
    give(1, 1)
    add_up(0, 2)
    exchange_far(1)
    exchange_near(0)
    exchange_near(1)
    some = pl.ds(1, members - 1)
    for half in range(halves):
        for role in range(2):
            wait_for(cols.at[half, role, theirs], b_send.at[half, role])
            wait_for(rows.at[half, role, 0], y_send.at[half, role, 0])
        for behind in range(reps):
            wait_for(relay.at[half, 0, some], a_send.at[half, behind])
        wait_for(landed.at[half, :, some, stages[0]], r_send.at[half, 0])
    for stage in (1, 2):
        wait_for(landed.at[0, :, some, stages[stage]], r_send.at[0, stage])
        for role in range(2):
            wait_for(rows.at[0, role, 0], y_send.at[0, role, stage])
    multiply_far(0)
    give_far()
    add_up(1, 1)
    wait_for(placed.at[pl.ds(0, reps - 1)], o_recv.at[0])
    finish(0)
    multiply_far(1)
    for role in range(2):
        give_direct(role, 3, 1)
    for role in range(2):
        multiply_near(role, 0)
    for role in range(2):
        multiply_near(role, 1)
        give_direct(role, 0, 0)
    add_up_far()
    for role in range(2):
        wait_for(rows.at[1, role, 0], y_send.at[1, role, 1])
        for index in range(2):
            wait_for(rows.at[1, role, 0, far_pieces[index]], p_send.at[role, index])
            wait_for(rows.at[1, role, 0, near, :, stretches[index]], p_send.at[role, 2 + index])
        for slot in range(3):
            wait_for(summed.at[0, role, slot], o_send.at[0, role, slot])
        for slot in range(2):
            wait_for(summed.at[1, role, slot], o_send.at[1, role, slot])
    wait_for(landed.at[1, :, some, stages[1]], r_send.at[1, 1])
    wait_for(landed.at[1, :, far_pieces[0], 3], l_send)
    for role in range(2):
        wait_for(direct.at[role], d_send.at[role])
        wait_for(direct.at[role], d_recv.at[role])
        wait_for(summed.at[1, role, 2], o_send.at[1, role, 2])
    wait_for(placed.at[pl.ds(reps, reps - 1)], o_recv.at[1])
    for role, behind in ((0, 1), (1, 0)):
        g = irrep(behind, 1)
        placed[g, role] = placed[g, role] + jnp.sum(direct[role], axis=(0, 1))
    finish(1)


def per_device(reps, members, amplitudes, integrals, live_pairs):
    irreps, blocks, owned, depth = amplitudes.shape
    cuts = integrals.shape[1]
    halves = irreps // reps
    dma = pltpu.SemaphoreType.DMA
    f32, bf16 = jnp.float32, jnp.bfloat16
    sums = pl.pallas_call(
        functools.partial(ladder_kernel, reps, members),
        out_shape=jax.ShapeDtypeStruct((irreps, owned, reps * cuts), bf16),
        in_specs=[pl.BlockSpec(memory_space=pl.ANY)] * 2,
        out_specs=pl.BlockSpec(memory_space=pltpu.VMEM),
        scratch_shapes=[
            pltpu.VMEM((halves, 2, 4, members, owned, depth), bf16),
            pltpu.VMEM((halves, 2, members, owned, depth), bf16),
            pltpu.VMEM((halves, 2, 2 * cuts, depth), bf16),
            pltpu.VMEM((halves, 2, members, 4, owned, 2 * cuts), f32),
            pltpu.VMEM((halves, 2, members, 4, owned, 2 * cuts), f32),
            pltpu.VMEM((halves, 2, 4, owned, 2 * cuts), f32),
            pltpu.VMEM((irreps, 2, owned, 2 * cuts), f32),
            pltpu.VMEM((2, 2, GROUP, owned, 2 * cuts), f32),
            dma((halves, 2)), dma((halves, 2)), dma((halves, 2)),
            dma((halves, 4)), dma((halves, 4)),
            dma((halves, 2, 3)), dma((halves, 2, 3)),
            dma((2, 4)), dma((2, 4)),
            dma((halves, 3)), dma((halves, 3)),
            dma, dma,
            dma((halves, 2, 3)), dma((halves,)),
            dma((2,)), dma((2,)),
        ],
        compiler_params=pltpu.CompilerParams(collective_id=0, has_side_effects=True, vmem_limit_bytes=52 * MIB),
        cost_estimate=pl.CostEstimate(
            flops=2 * irreps * owned * members * 4 * cuts * depth, bytes_accessed=26 * MIB, transcendentals=0
        ),
        name="ladder",
    )(amplitudes, integrals)
    sums, live_pairs = lax.optimization_barrier((sums, live_pairs))
    first = (lax.axis_index("rep") * members + lax.axis_index("wide")) * owned
    index = first + lax.broadcasted_iota(jnp.int32, sums.shape, 1)
    return jnp.where(index < live_pairs[:, None, None], sums, jnp.zeros_like(sums))


def solution(mesh):
    in_specs = (P(None, None, ("rep", "wide"), None), P(None, "rep", "wide"), P())
    out_specs = P(None, ("rep", "wide"), None)
    return jax.shard_map(
        functools.partial(per_device, mesh.shape["rep"], mesh.shape["wide"]),
        mesh=mesh, in_specs=in_specs, out_specs=out_specs, check_vma=False,
    )
```

```python
import functools

import jax
import jax.numpy as jnp
from jax import lax
from jax.experimental import pallas as pl
from jax.experimental.pallas import tpu as pltpu
from jax.sharding import PartitionSpec as P

MESH = pl.DeviceIdType.MESH
MIB = 2**20
GROUP = 8


def ladder_kernel(reps, members, amp, integ, out, rows, relay, cols, part, landed, summed, placed, direct,
                  b_send, b_recv, b_own, a_send, a_recv, y_send, y_recv, p_send, p_recv,
                  r_send, r_recv, l_send, l_recv, o_send, o_recv, d_send, d_recv, ready):
    r, w = lax.axis_index("rep"), lax.axis_index("wide")
    up, down, across = (r + 1) % reps, (r + reps - 1) % reps, (r + 2) % reps
    groups = members // GROUP
    plane, seat = w // GROUP, w % GROUP
    cuts = integ.shape[1]
    owned, depth = amp.shape[2], amp.shape[3]
    halves = amp.shape[0] // reps
    beside = {1: (down, up), 2: (across, across), 3: (up, down)}

    def irrep(behind, half):
        return (r + reps - behind) % reps + reps * half

    def remote(src, dst, send, recv, rep, member):
        return pltpu.make_async_remote_copy(
            src_ref=src, dst_ref=dst, send_sem=send, recv_sem=recv, device_id=(rep, member), device_id_type=MESH
        )

    def wait_for(ref, sem):
        pltpu.make_async_copy(ref, ref, sem).wait()

    def other(t):
        return (w + t) % members

    barrier = pltpu.get_barrier_semaphore()

    def greet(rep, member):
        pl.semaphore_signal(barrier, inc=1, device_id=(rep, member), device_id_type=MESH)

    greet(up, w)
    greet(down, w)
    for t in range(1, GROUP):
        greet(r, plane * GROUP + (seat + t) % GROUP)

    def each_after(act):
        for step in range(1, groups):
            @pl.when(plane + step < groups)
            def _():
                act(w + step * GROUP)

    def each_before(act):
        for step in range(1, groups):
            @pl.when(plane >= step)
            def _():
                act(w - step * GROUP)

    def tell(sem):
        def one(member):
            pl.semaphore_signal(sem, inc=1, device_id=(r, member), device_id_type=MESH)

        return one

    each_after(functools.partial(greet, r))
    pl.semaphore_wait(barrier, GROUP + 1 + plane)

    def meet_plane():
        each_before(tell(ready.at[0]))

        @pl.when(plane < groups - 1)
        def _():
            pl.semaphore_wait(ready.at[0], groups - 1 - plane)

        each_after(tell(ready.at[1]))

        @pl.when(plane > 0)
        def _():
            pl.semaphore_wait(ready.at[1], plane)

    mine, theirs = pl.ds(0, cuts), pl.ds(cuts, cuts)
    near = pl.ds(0, GROUP)
    far_steps = ((1, 2), (3,))
    far_pieces = (pl.ds(GROUP, 2 * GROUP), pl.ds(3 * GROUP, GROUP))
    stretches = (pl.ds(0, depth // 2), pl.ds(depth // 2, depth // 2))

    def send_columns(half):
        remote(integ.at[irrep(3, half)], cols.at[half, 0, theirs], b_send.at[half, 0], b_recv.at[half, 0], up, w).start()
        remote(integ.at[irrep(2, half)], cols.at[half, 1, theirs], b_send.at[half, 1], b_recv.at[half, 1], down, w).start()

    def own_columns(half, role):
        return pltpu.make_async_copy(integ.at[irrep(role, half)], cols.at[half, role, mine], b_own.at[half, role])

    def columns_ready(half):
        for role in range(2):
            own_columns(half, role).wait()
            wait_for(cols.at[half, role, theirs], b_recv.at[half, role])

    def arriving(behind, half):
        return rows.at[half, behind, 0] if behind < 2 else relay.at[half, behind - 2]

    def spread(behind, half):
        g, target = irrep(behind, half), arriving(behind, half)
        send, recv = a_send.at[half, behind], a_recv.at[half, behind]
        pltpu.make_async_copy(amp.at[g, w], target.at[w], recv).start()

        def one(t, carry):
            remote(amp.at[g, other(t)], target.at[w], send, recv, r, other(t)).start()
            return carry

        lax.fori_loop(1, members, one, 0)

    def arrived(behind, half):
        wait_for(arriving(behind, half), a_recv.at[half, behind])

    def along(src, half, role, slot, rep):
        return remote(src, rows.at[half, role, slot], y_send.at[half, role, slot - 1], y_recv.at[half, role, slot - 1],
                      rep, w)

    def relay_rows(half):
        arrived(3, half)
        along(relay.at[half, 1], half, 0, 1, up).start()
        arrived(2, half)
        along(relay.at[half, 0], half, 1, 1, down).start()

    def forward_rows(half):
        took(half, 0, 1)
        along(rows.at[half, 0, 1], half, 1, 2, up).start()
        took(half, 1, 1)
        along(rows.at[half, 1, 1], half, 0, 2, down).start()

    def exchange_rows(half):
        arrived(0, half)
        along(rows.at[half, 0, 0], half, 1, 3, up).start()
        arrived(1, half)
        along(rows.at[half, 1, 0], half, 0, 3, down).start()

    def took(half, role, slot):
        wait_for(rows.at[half, role, slot], y_recv.at[half, role, slot - 1])

    def group_at(step):
        return pl.ds((plane + step) % groups * GROUP, GROUP)

    def exchange_far(piece):
        for role, rep in ((0, up), (1, down)):
            for step in far_steps[piece]:
                remote(rows.at[1, role, 0, group_at(step)], rows.at[1, 1 - role, 3, pl.ds(step * GROUP, GROUP)],
                       p_send.at[role, piece], p_recv.at[1 - role, piece], rep, w).start()

    def exchange_near(stretch):
        for role, rep in ((0, up), (1, down)):
            remote(rows.at[1, role, 0, group_at(0), :, stretches[stretch]], rows.at[1, 1 - role, 3, near, :, stretches[stretch]],
                   p_send.at[role, 2 + stretch], p_recv.at[1 - role, 2 + stretch], rep, w).start()

    def product(left, half, role):
        return lax.dot_general(left, cols[half, role], (((1,), (1,)), ((), ())), preferred_element_type=jnp.float32)

    def multiply(half, role, slot):
        left = rows[half, role, slot].reshape(members * owned, depth)
        part[half, role, :, slot] = product(left, half, role).reshape(members, owned, 2 * cuts)

    def multiply_far(piece):
        at = far_pieces[piece]
        for role in range(2):
            wait_for(rows.at[1, role, 3, at], p_recv.at[role, piece])
            left = rows[1, role, 3, at].reshape(at.size * owned, depth)
            part[1, role, at, 3] = product(left, 1, role).reshape(at.size, owned, 2 * cuts)

    def multiply_near(role, stretch):
        inner = stretches[stretch]
        wait_for(rows.at[1, role, 3, near, :, inner], p_recv.at[role, 2 + stretch])
        left = rows[1, role, 3, near, :, inner].reshape(GROUP * owned, depth // 2)
        some = lax.dot_general(
            left, cols[1, role, :, inner], (((1,), (1,)), ((), ())), preferred_element_type=jnp.float32
        ).reshape(GROUP, owned, 2 * cuts)
        part[1, role, near, 3] = some if stretch == 0 else part[1, role, near, 3] + some

    stages = (pl.ds(0, 2), pl.ds(2, 1), pl.ds(3, 1))

    def give(half, stage):
        slots, send, recv = stages[stage], r_send.at[half, stage], r_recv.at[half, stage]
        pltpu.make_async_copy(part.at[half, :, w, slots], landed.at[half, :, w, slots], recv).start()

        def one(t, carry):
            remote(
                part.at[half, :, other(t), slots], landed.at[half, :, w, slots], send, recv, r, other(t)
            ).start()
            return carry

        lax.fori_loop(1, members, one, 0)

    def give_far():
        def one(t, carry):
            step, place = t // GROUP, (seat + t) % GROUP
            member = (plane + step) % groups * GROUP + place
            remote(part.at[1, :, step * GROUP + place, 3], landed.at[1, :, step * GROUP + seat, 3], l_send, l_recv,
                   r, member).start()
            return carry

        at = far_pieces[0]
        lax.fori_loop(at.start, at.start + at.size, one, 0)

    def give_direct(role, step, kept):
        def one(t, carry):
            place = (seat + t) % GROUP
            remote(part.at[1, role, step * GROUP + place, 3], direct.at[role, kept, seat], d_send.at[role],
                   d_recv.at[role], beside[3][role], (plane + step) % groups * GROUP + place).start()
            return carry

        lax.fori_loop(0, GROUP, one, 0)

    def add_up(half, stage):
        slots = stages[stage]
        wait_for(landed.at[half, :, :, slots], r_recv.at[half, stage])
        summed[half, :, slots] = jnp.sum(landed[half, :, :, slots], axis=1)
        hand_out(half, ((0, 1), (2,), (3,))[stage])

    def add_up_far():
        wait_for(landed.at[1, :, far_pieces[0], 3], l_recv)
        summed[1, :, 3] = jnp.sum(landed[1, :, far_pieces[0], 3], axis=1)
        hand_out(1, (3,))

    def hand_out(half, slots):
        for role in range(2):
            g = irrep(role, half)
            for slot in slots:
                if slot == 0:
                    placed[g, role] = summed[half, role, 0]
                else:
                    remote(summed.at[half, role, slot], placed.at[g, role], o_send.at[half, role, slot - 1],
                           o_recv.at[half], beside[slot][role], w).start()

    def finish(half):
        for p in range(reps):
            g = reps * half + p
            found = {}
            for role, beyond in ((0, reps - 1), (1, 1)):
                here = (p + role) % reps
                found[here] = placed[g, role, :, :cuts]
                found[(here + beyond) % reps] = placed[g, role, :, cuts:]
            out[g] = jnp.concatenate([found[q] for q in range(reps)], axis=1).astype(out.dtype)

    send_columns(0)
    send_columns(1)
    meet_plane()
    spread(3, 0)
    spread(2, 0)
    for half in range(halves):
        for role in range(2):
            own_columns(half, role).start()
    spread(3, 1)
    spread(2, 1)
    relay_rows(0)
    spread(0, 0)
    spread(1, 0)
    relay_rows(1)
    spread(0, 1)
    spread(1, 1)
    forward_rows(0)
    exchange_rows(0)

    columns_ready(0)
    for role in range(2):
        multiply(0, role, 0)
        multiply(0, role, 1)
    give(0, 0)
    forward_rows(1)
    arrived(0, 1)
    arrived(1, 1)
    add_up(0, 0)
    columns_ready(1)
    for role in range(2):
        multiply(1, role, 0)
        multiply(1, role, 1)
    give(1, 0)
    for role in range(2):
        took(0, role, 2)
        multiply(0, role, 2)
    give(0, 1)
    add_up(1, 0)
    for role in range(2):
        took(0, role, 3)
        multiply(0, role, 3)
    give(0, 2)
    add_up(0, 1)
    exchange_far(0)
    for role in range(2):
        took(1, role, 2)
        multiply(1, role, 2)
    give(1, 1)
    add_up(0, 2)
    exchange_far(1)
    exchange_near(0)
    exchange_near(1)
    some = pl.ds(1, members - 1)
    for half in range(halves):
        for role in range(2):
            wait_for(cols.at[half, role, theirs], b_send.at[half, role])
            wait_for(rows.at[half, role, 0], y_send.at[half, role, 0])
        for behind in range(reps):
            wait_for(relay.at[half, 0, some], a_send.at[half, behind])
        wait_for(landed.at[half, :, some, stages[0]], r_send.at[half, 0])
    for stage in (1, 2):
        wait_for(landed.at[0, :, some, stages[stage]], r_send.at[0, stage])
        for role in range(2):
            wait_for(rows.at[0, role, 0], y_send.at[0, role, stage])
    multiply_far(0)
    give_far()
    multiply_far(1)
    for role in range(2):
        give_direct(role, 3, 1)
    for role in range(2):
        multiply_near(role, 0)
    for role in range(2):
        multiply_near(role, 1)
        give_direct(role, 0, 0)
    add_up(1, 1)
    wait_for(placed.at[pl.ds(0, reps - 1)], o_recv.at[0])
    finish(0)
    add_up_far()
    for role in range(2):
        wait_for(rows.at[1, role, 0], y_send.at[1, role, 1])
        for index in range(2):
            wait_for(rows.at[1, role, 0, far_pieces[index]], p_send.at[role, index])
            wait_for(rows.at[1, role, 0, near, :, stretches[index]], p_send.at[role, 2 + index])
        for slot in range(3):
            wait_for(summed.at[0, role, slot], o_send.at[0, role, slot])
        for slot in range(2):
            wait_for(summed.at[1, role, slot], o_send.at[1, role, slot])
    wait_for(landed.at[1, :, some, stages[1]], r_send.at[1, 1])
    wait_for(landed.at[1, :, far_pieces[0], 3], l_send)
    for role in range(2):
        wait_for(direct.at[role], d_send.at[role])
        wait_for(direct.at[role], d_recv.at[role])
        wait_for(summed.at[1, role, 2], o_send.at[1, role, 2])
    wait_for(placed.at[pl.ds(reps, reps - 1)], o_recv.at[1])
    for role, behind in ((0, 1), (1, 0)):
        g = irrep(behind, 1)
        placed[g, role] = placed[g, role] + jnp.sum(direct[role], axis=(0, 1))
    finish(1)


def per_device(reps, members, amplitudes, integrals, live_pairs):
    irreps, blocks, owned, depth = amplitudes.shape
    cuts = integrals.shape[1]
    halves = irreps // reps
    dma = pltpu.SemaphoreType.DMA
    f32, bf16 = jnp.float32, jnp.bfloat16
    sums = pl.pallas_call(
        functools.partial(ladder_kernel, reps, members),
        out_shape=jax.ShapeDtypeStruct((irreps, owned, reps * cuts), bf16),
        in_specs=[pl.BlockSpec(memory_space=pl.ANY)] * 2,
        out_specs=pl.BlockSpec(memory_space=pltpu.VMEM),
        scratch_shapes=[
            pltpu.VMEM((halves, 2, 4, members, owned, depth), bf16),
            pltpu.VMEM((halves, 2, members, owned, depth), bf16),
            pltpu.VMEM((halves, 2, 2 * cuts, depth), bf16),
            pltpu.VMEM((halves, 2, members, 4, owned, 2 * cuts), f32),
            pltpu.VMEM((halves, 2, members, 4, owned, 2 * cuts), f32),
            pltpu.VMEM((halves, 2, 4, owned, 2 * cuts), f32),
            pltpu.VMEM((irreps, 2, owned, 2 * cuts), f32),
            pltpu.VMEM((2, 2, GROUP, owned, 2 * cuts), f32),
            dma((halves, 2)), dma((halves, 2)), dma((halves, 2)),
            dma((halves, 4)), dma((halves, 4)),
            dma((halves, 2, 3)), dma((halves, 2, 3)),
            dma((2, 4)), dma((2, 4)),
            dma((halves, 3)), dma((halves, 3)),
            dma, dma,
            dma((halves, 2, 3)), dma((halves,)),
            dma((2,)), dma((2,)), pltpu.SemaphoreType.REGULAR((2,)),
        ],
        compiler_params=pltpu.CompilerParams(collective_id=0, has_side_effects=True, vmem_limit_bytes=52 * MIB),
        cost_estimate=pl.CostEstimate(
            flops=2 * irreps * owned * members * 4 * cuts * depth, bytes_accessed=26 * MIB, transcendentals=0
        ),
        name="ladder",
    )(amplitudes, integrals)
    sums, live_pairs = lax.optimization_barrier((sums, live_pairs))
    first = (lax.axis_index("rep") * members + lax.axis_index("wide")) * owned
    index = first + lax.broadcasted_iota(jnp.int32, sums.shape, 1)
    return jnp.where(index < live_pairs[:, None, None], sums, jnp.zeros_like(sums))


def solution(mesh):
    in_specs = (P(None, None, ("rep", "wide"), None), P(None, "rep", "wide"), P())
    out_specs = P(None, ("rep", "wide"), None)
    return jax.shard_map(
        functools.partial(per_device, mesh.shape["rep"], mesh.shape["wide"]),
        mesh=mesh, in_specs=in_specs, out_specs=out_specs, check_vma=False,
    )
```

```python
import functools

import jax
import jax.numpy as jnp
from jax import lax
from jax.experimental import pallas as pl
from jax.experimental.pallas import tpu as pltpu
from jax.sharding import PartitionSpec as P

MESH = pl.DeviceIdType.MESH
MIB = 2**20
GROUP = 8


def ladder_kernel(reps, members, amp, integ, out, rows, relay, cols, part, landed, summed, placed, direct,
                  b_send, b_recv, b_own, a_send, a_recv, y_send, y_recv, p_send, p_recv,
                  r_send, r_recv, l_send, l_recv, o_send, o_recv, d_send, d_recv, ready):
    r, w = lax.axis_index("rep"), lax.axis_index("wide")
    up, down, across = (r + 1) % reps, (r + reps - 1) % reps, (r + 2) % reps
    groups = members // GROUP
    plane, seat = w // GROUP, w % GROUP
    cuts = integ.shape[1]
    owned, depth = amp.shape[2], amp.shape[3]
    halves = amp.shape[0] // reps
    beside = {1: (down, up), 2: (across, across), 3: (up, down)}

    def irrep(behind, half):
        return (r + reps - behind) % reps + reps * half

    def remote(src, dst, send, recv, rep, member):
        return pltpu.make_async_remote_copy(
            src_ref=src, dst_ref=dst, send_sem=send, recv_sem=recv, device_id=(rep, member), device_id_type=MESH
        )

    def wait_for(ref, sem):
        pltpu.make_async_copy(ref, ref, sem).wait()

    def other(t):
        return (w + t) % members

    barrier = pltpu.get_barrier_semaphore()

    def greet(rep, member):
        pl.semaphore_signal(barrier, inc=1, device_id=(rep, member), device_id_type=MESH)

    greet(up, w)
    greet(down, w)
    for t in range(1, GROUP):
        greet(r, plane * GROUP + (seat + t) % GROUP)

    def each_after(act):
        for step in range(1, groups):
            @pl.when(plane + step < groups)
            def _():
                act(w + step * GROUP)

    def each_before(act):
        for step in range(1, groups):
            @pl.when(plane >= step)
            def _():
                act(w - step * GROUP)

    def tell(sem):
        def one(member):
            pl.semaphore_signal(sem, inc=1, device_id=(r, member), device_id_type=MESH)

        return one

    each_after(functools.partial(greet, r))
    pl.semaphore_wait(barrier, GROUP + 1 + plane)

    def meet_plane():
        each_before(tell(ready.at[0]))

        @pl.when(plane < groups - 1)
        def _():
            pl.semaphore_wait(ready.at[0], groups - 1 - plane)

        each_after(tell(ready.at[1]))

        @pl.when(plane > 0)
        def _():
            pl.semaphore_wait(ready.at[1], plane)

    mine, theirs = pl.ds(0, cuts), pl.ds(cuts, cuts)
    near = pl.ds(0, GROUP)
    far_planes = (2, 1, 3)
    far_pieces = tuple(pl.ds((k + 1) * GROUP, GROUP) for k in range(3))
    stretches = (pl.ds(0, depth // 2), pl.ds(depth // 2, depth // 2))

    def send_columns(half):
        remote(integ.at[irrep(3, half)], cols.at[half, 0, theirs], b_send.at[half, 0], b_recv.at[half, 0], up, w).start()
        remote(integ.at[irrep(2, half)], cols.at[half, 1, theirs], b_send.at[half, 1], b_recv.at[half, 1], down, w).start()

    def own_columns(half, role):
        return pltpu.make_async_copy(integ.at[irrep(role, half)], cols.at[half, role, mine], b_own.at[half, role])

    def columns_ready(half):
        for role in range(2):
            own_columns(half, role).wait()
            wait_for(cols.at[half, role, theirs], b_recv.at[half, role])

    def arriving(behind, half):
        return rows.at[half, behind, 0] if behind < 2 else relay.at[half, behind - 2]

    def spread(behind, half):
        g, target = irrep(behind, half), arriving(behind, half)
        send, recv = a_send.at[half, behind], a_recv.at[half, behind]
        pltpu.make_async_copy(amp.at[g, w], target.at[w], recv).start()

        def one(t, carry):
            remote(amp.at[g, other(t)], target.at[w], send, recv, r, other(t)).start()
            return carry

        lax.fori_loop(1, members, one, 0)

    def arrived(behind, half):
        wait_for(arriving(behind, half), a_recv.at[half, behind])

    def along(src, half, role, slot, rep):
        return remote(src, rows.at[half, role, slot], y_send.at[half, role, slot - 1], y_recv.at[half, role, slot - 1],
                      rep, w)

    def relay_rows(half):
        arrived(3, half)
        along(relay.at[half, 1], half, 0, 1, up).start()
        arrived(2, half)
        along(relay.at[half, 0], half, 1, 1, down).start()

    def forward_rows(half):
        took(half, 0, 1)
        along(rows.at[half, 0, 1], half, 1, 2, up).start()
        took(half, 1, 1)
        along(rows.at[half, 1, 1], half, 0, 2, down).start()

    def exchange_rows(half):
        arrived(0, half)
        along(rows.at[half, 0, 0], half, 1, 3, up).start()
        arrived(1, half)
        along(rows.at[half, 1, 0], half, 0, 3, down).start()

    def took(half, role, slot):
        wait_for(rows.at[half, role, slot], y_recv.at[half, role, slot - 1])

    def group_at(step):
        return pl.ds((plane + step) % groups * GROUP, GROUP)

    def exchange_far(piece):
        for role, rep in ((0, up), (1, down)):
            remote(rows.at[1, role, 0, group_at(far_planes[piece])], rows.at[1, 1 - role, 3, far_pieces[piece]],
                   p_send.at[role, piece], p_recv.at[1 - role, piece], rep, w).start()

    def exchange_near(stretch):
        for role, rep in ((0, up), (1, down)):
            remote(rows.at[1, role, 0, group_at(0), :, stretches[stretch]], rows.at[1, 1 - role, 3, near, :, stretches[stretch]],
                   p_send.at[role, 3 + stretch], p_recv.at[1 - role, 3 + stretch], rep, w).start()

    def product(left, half, role):
        return lax.dot_general(left, cols[half, role], (((1,), (1,)), ((), ())), preferred_element_type=jnp.float32)

    def multiply(half, role, slot):
        left = rows[half, role, slot].reshape(members * owned, depth)
        part[half, role, :, slot] = product(left, half, role).reshape(members, owned, 2 * cuts)

    def multiply_far(piece):
        at = far_pieces[piece]
        for role in range(2):
            wait_for(rows.at[1, role, 3, at], p_recv.at[role, piece])
            left = rows[1, role, 3, at].reshape(at.size * owned, depth)
            part[1, role, at, 3] = product(left, 1, role).reshape(at.size, owned, 2 * cuts)

    def multiply_near(role, stretch):
        inner = stretches[stretch]
        wait_for(rows.at[1, role, 3, near, :, inner], p_recv.at[role, 3 + stretch])
        left = rows[1, role, 3, near, :, inner].reshape(GROUP * owned, depth // 2)
        some = lax.dot_general(
            left, cols[1, role, :, inner], (((1,), (1,)), ((), ())), preferred_element_type=jnp.float32
        ).reshape(GROUP, owned, 2 * cuts)
        part[1, role, near, 3] = some if stretch == 0 else part[1, role, near, 3] + some

    stages = (pl.ds(0, 2), pl.ds(2, 1), pl.ds(3, 1))

    def give(half, stage):
        slots, send, recv = stages[stage], r_send.at[half, stage], r_recv.at[half, stage]
        pltpu.make_async_copy(part.at[half, :, w, slots], landed.at[half, :, w, slots], recv).start()

        def one(t, carry):
            remote(
                part.at[half, :, other(t), slots], landed.at[half, :, w, slots], send, recv, r, other(t)
            ).start()
            return carry

        lax.fori_loop(1, members, one, 0)

    def give_far(piece):
        place, base = far_pieces[piece].start, (plane + far_planes[piece]) % groups * GROUP

        def one(t, carry):
            there = (seat + t) % GROUP
            remote(part.at[1, :, place + there, 3], landed.at[1, :, place + seat, 3], l_send, l_recv,
                   r, base + there).start()
            return carry

        lax.fori_loop(0, GROUP, one, 0)

    def give_direct(role, place, step, kept):
        base = (plane + step) % groups * GROUP

        def one(t, carry):
            there = (seat + t) % GROUP
            remote(part.at[1, role, place * GROUP + there, 3], direct.at[role, kept, seat], d_send.at[role],
                   d_recv.at[role], beside[3][role], base + there).start()
            return carry

        lax.fori_loop(0, GROUP, one, 0)

    def add_up(half, stage):
        slots = stages[stage]
        wait_for(landed.at[half, :, :, slots], r_recv.at[half, stage])
        summed[half, :, slots] = jnp.sum(landed[half, :, :, slots], axis=1)
        hand_out(half, ((0, 1), (2,), (3,))[stage])

    def add_up_far():
        wait_for(landed.at[1, :, pl.ds(GROUP, 2 * GROUP), 3], l_recv)
        summed[1, :, 3] = jnp.sum(landed[1, :, pl.ds(GROUP, 2 * GROUP), 3], axis=1)
        hand_out(1, (3,))

    def hand_out(half, slots):
        for role in range(2):
            g = irrep(role, half)
            for slot in slots:
                if slot == 0:
                    placed[g, role] = summed[half, role, 0]
                else:
                    remote(summed.at[half, role, slot], placed.at[g, role], o_send.at[half, role, slot - 1],
                           o_recv.at[half], beside[slot][role], w).start()

    def finish(half):
        for p in range(reps):
            g = reps * half + p
            found = {}
            for role, beyond in ((0, reps - 1), (1, 1)):
                here = (p + role) % reps
                found[here] = placed[g, role, :, :cuts]
                found[(here + beyond) % reps] = placed[g, role, :, cuts:]
            out[g] = jnp.concatenate([found[q] for q in range(reps)], axis=1).astype(out.dtype)

    send_columns(0)
    send_columns(1)
    meet_plane()
    spread(3, 0)
    spread(2, 0)
    for half in range(halves):
        for role in range(2):
            own_columns(half, role).start()
    spread(3, 1)
    spread(2, 1)
    relay_rows(0)
    spread(0, 0)
    spread(1, 0)
    relay_rows(1)
    spread(0, 1)
    spread(1, 1)
    forward_rows(0)
    exchange_rows(0)

    columns_ready(0)
    for role in range(2):
        multiply(0, role, 0)
        multiply(0, role, 1)
    give(0, 0)
    forward_rows(1)
    arrived(0, 1)
    arrived(1, 1)
    add_up(0, 0)
    columns_ready(1)
    for role in range(2):
        multiply(1, role, 0)
        multiply(1, role, 1)
    give(1, 0)
    for role in range(2):
        took(0, role, 2)
        multiply(0, role, 2)
    give(0, 1)
    add_up(1, 0)
    for role in range(2):
        took(0, role, 3)
        multiply(0, role, 3)
    give(0, 2)
    add_up(0, 1)
    exchange_far(0)
    exchange_far(1)
    for role in range(2):
        took(1, role, 2)
        multiply(1, role, 2)
    give(1, 1)
    add_up(0, 2)
    exchange_far(2)
    exchange_near(0)
    exchange_near(1)
    some = pl.ds(1, members - 1)
    for half in range(halves):
        for role in range(2):
            wait_for(cols.at[half, role, theirs], b_send.at[half, role])
            wait_for(rows.at[half, role, 0], y_send.at[half, role, 0])
        for behind in range(reps):
            wait_for(relay.at[half, 0, some], a_send.at[half, behind])
        wait_for(landed.at[half, :, some, stages[0]], r_send.at[half, 0])
    for stage in (1, 2):
        wait_for(landed.at[0, :, some, stages[stage]], r_send.at[0, stage])
        for role in range(2):
            wait_for(rows.at[0, role, 0], y_send.at[0, role, stage])
    for piece in range(2):
        multiply_far(piece)
        give_far(piece)
    multiply_far(2)
    for role in range(2):
        give_direct(role, 3, 3, 1)
    for role in range(2):
        multiply_near(role, 0)
    for role in range(2):
        multiply_near(role, 1)
        give_direct(role, 0, 0, 0)
    add_up(1, 1)
    wait_for(placed.at[pl.ds(0, reps - 1)], o_recv.at[0])
    finish(0)
    add_up_far()
    for role in range(2):
        wait_for(rows.at[1, role, 0], y_send.at[1, role, 1])
        for index in range(3):
            wait_for(rows.at[1, role, 0, far_pieces[index]], p_send.at[role, index])
        for index in range(2):
            wait_for(rows.at[1, role, 0, near, :, stretches[index]], p_send.at[role, 3 + index])
        for slot in range(3):
            wait_for(summed.at[0, role, slot], o_send.at[0, role, slot])
        for slot in range(2):
            wait_for(summed.at[1, role, slot], o_send.at[1, role, slot])
    wait_for(landed.at[1, :, some, stages[1]], r_send.at[1, 1])
    wait_for(landed.at[1, :, pl.ds(GROUP, 2 * GROUP), 3], l_send)
    for role in range(2):
        wait_for(direct.at[role], d_send.at[role])
        wait_for(direct.at[role], d_recv.at[role])
        wait_for(summed.at[1, role, 2], o_send.at[1, role, 2])
    wait_for(placed.at[pl.ds(reps, reps - 1)], o_recv.at[1])
    for role, behind in ((0, 1), (1, 0)):
        g = irrep(behind, 1)
        placed[g, role] = placed[g, role] + jnp.sum(direct[role], axis=(0, 1))
    finish(1)


def per_device(reps, members, amplitudes, integrals, live_pairs):
    irreps, blocks, owned, depth = amplitudes.shape
    cuts = integrals.shape[1]
    halves = irreps // reps
    dma = pltpu.SemaphoreType.DMA
    f32, bf16 = jnp.float32, jnp.bfloat16
    sums = pl.pallas_call(
        functools.partial(ladder_kernel, reps, members),
        out_shape=jax.ShapeDtypeStruct((irreps, owned, reps * cuts), bf16),
        in_specs=[pl.BlockSpec(memory_space=pl.ANY)] * 2,
        out_specs=pl.BlockSpec(memory_space=pltpu.VMEM),
        scratch_shapes=[
            pltpu.VMEM((halves, 2, 4, members, owned, depth), bf16),
            pltpu.VMEM((halves, 2, members, owned, depth), bf16),
            pltpu.VMEM((halves, 2, 2 * cuts, depth), bf16),
            pltpu.VMEM((halves, 2, members, 4, owned, 2 * cuts), f32),
            pltpu.VMEM((halves, 2, members, 4, owned, 2 * cuts), f32),
            pltpu.VMEM((halves, 2, 4, owned, 2 * cuts), f32),
            pltpu.VMEM((irreps, 2, owned, 2 * cuts), f32),
            pltpu.VMEM((2, 2, GROUP, owned, 2 * cuts), f32),
            dma((halves, 2)), dma((halves, 2)), dma((halves, 2)),
            dma((halves, 4)), dma((halves, 4)),
            dma((halves, 2, 3)), dma((halves, 2, 3)),
            dma((2, 5)), dma((2, 5)),
            dma((halves, 3)), dma((halves, 3)),
            dma, dma,
            dma((halves, 2, 3)), dma((halves,)),
            dma((2,)), dma((2,)), pltpu.SemaphoreType.REGULAR((2,)),
        ],
        compiler_params=pltpu.CompilerParams(collective_id=0, has_side_effects=True, vmem_limit_bytes=52 * MIB),
        cost_estimate=pl.CostEstimate(
            flops=2 * irreps * owned * members * 4 * cuts * depth, bytes_accessed=26 * MIB, transcendentals=0
        ),
        name="ladder",
    )(amplitudes, integrals)
    sums, live_pairs = lax.optimization_barrier((sums, live_pairs))
    first = (lax.axis_index("rep") * members + lax.axis_index("wide")) * owned
    index = first + lax.broadcasted_iota(jnp.int32, sums.shape, 1)
    return jnp.where(index < live_pairs[:, None, None], sums, jnp.zeros_like(sums))


def solution(mesh):
    in_specs = (P(None, None, ("rep", "wide"), None), P(None, "rep", "wide"), P())
    out_specs = P(None, ("rep", "wide"), None)
    return jax.shard_map(
        functools.partial(per_device, mesh.shape["rep"], mesh.shape["wide"]),
        mesh=mesh, in_specs=in_specs, out_specs=out_specs, check_vma=False,
    )
```

```python
import functools

import jax
import jax.numpy as jnp
from jax import lax
from jax.experimental import pallas as pl
from jax.experimental.pallas import tpu as pltpu
from jax.sharding import PartitionSpec as P

MESH = pl.DeviceIdType.MESH
MIB = 2**20
GROUP = 8


def ladder_kernel(reps, members, amp, integ, out, rows, relay, cols, part, landed, handed, placed, last, late, direct,
                  b_send, b_recv, b_own, a_send, a_recv, y_send, y_recv, p_send, p_recv,
                  r_send, r_recv, l_send, l_recv, o_send, o_recv, d_send, d_recv, late_recv, ready):
    r, w = lax.axis_index("rep"), lax.axis_index("wide")
    up, down, across = (r + 1) % reps, (r + reps - 1) % reps, (r + 2) % reps
    groups = members // GROUP
    plane, seat = w // GROUP, w % GROUP
    cuts = integ.shape[1]
    owned, depth = amp.shape[2], amp.shape[3]
    halves = amp.shape[0] // reps
    beside = {1: (down, up), 2: (across, across), 3: (up, down)}

    def irrep(behind, half):
        return (r + reps - behind) % reps + reps * half

    def remote(src, dst, send, recv, rep, member):
        return pltpu.make_async_remote_copy(
            src_ref=src, dst_ref=dst, send_sem=send, recv_sem=recv, device_id=(rep, member), device_id_type=MESH
        )

    def wait_for(ref, sem):
        pltpu.make_async_copy(ref, ref, sem).wait()

    def other(t):
        return (w + t) % members

    barrier = pltpu.get_barrier_semaphore()

    def greet(rep, member):
        pl.semaphore_signal(barrier, inc=1, device_id=(rep, member), device_id_type=MESH)

    greet(up, w)
    greet(down, w)
    for t in range(1, GROUP):
        greet(r, plane * GROUP + (seat + t) % GROUP)

    def each_after(act):
        for step in range(1, groups):
            @pl.when(plane + step < groups)
            def _():
                act(w + step * GROUP)

    def each_before(act):
        for step in range(1, groups):
            @pl.when(plane >= step)
            def _():
                act(w - step * GROUP)

    def tell(sem):
        def one(member):
            pl.semaphore_signal(sem, inc=1, device_id=(r, member), device_id_type=MESH)

        return one

    each_after(functools.partial(greet, r))
    pl.semaphore_wait(barrier, GROUP + 1 + plane)

    def meet_plane():
        each_before(tell(ready.at[0]))

        @pl.when(plane < groups - 1)
        def _():
            pl.semaphore_wait(ready.at[0], groups - 1 - plane)

        each_after(tell(ready.at[1]))

        @pl.when(plane > 0)
        def _():
            pl.semaphore_wait(ready.at[1], plane)

    mine, theirs = pl.ds(0, cuts), pl.ds(cuts, cuts)
    near = pl.ds(0, GROUP)
    far_planes = (2, 1, 3)
    far_pieces = tuple(pl.ds((k + 1) * GROUP, GROUP) for k in range(3))
    stretches = pl.ds(0, depth * 7 // 10), pl.ds(depth * 7 // 10, depth * 3 // 10)

    def send_columns(half):
        remote(integ.at[irrep(3, half)], cols.at[half, 0, theirs], b_send.at[half, 0], b_recv.at[half, 0], up, w).start()
        remote(integ.at[irrep(2, half)], cols.at[half, 1, theirs], b_send.at[half, 1], b_recv.at[half, 1], down, w).start()

    def own_columns(half, role):
        return pltpu.make_async_copy(integ.at[irrep(role, half)], cols.at[half, role, mine], b_own.at[half, role])

    def columns_ready(half):
        for role in range(2):
            own_columns(half, role).wait()
            wait_for(cols.at[half, role, theirs], b_recv.at[half, role])

    def arriving(behind, half):
        return rows.at[half, behind, 0] if behind < 2 else relay.at[half, behind - 2]

    def spread(behind, half):
        g, target = irrep(behind, half), arriving(behind, half)
        send, recv = a_send.at[half, behind], a_recv.at[half, behind]
        pltpu.make_async_copy(amp.at[g, w], target.at[w], recv).start()

        def one(t, carry):
            remote(amp.at[g, other(t)], target.at[w], send, recv, r, other(t)).start()
            return carry

        lax.fori_loop(1, members, one, 0)

    def arrived(behind, half):
        wait_for(arriving(behind, half), a_recv.at[half, behind])

    def along(src, half, role, slot, rep):
        return remote(src, rows.at[half, role, slot], y_send.at[half, role, slot - 1], y_recv.at[half, role, slot - 1],
                      rep, w)

    def relay_rows(half):
        arrived(3, half)
        along(relay.at[half, 1], half, 0, 1, up).start()
        arrived(2, half)
        along(relay.at[half, 0], half, 1, 1, down).start()

    def forward_rows(half):
        took(half, 0, 1)
        along(rows.at[half, 0, 1], half, 1, 2, up).start()
        took(half, 1, 1)
        along(rows.at[half, 1, 1], half, 0, 2, down).start()

    def exchange_rows(half):
        arrived(0, half)
        along(rows.at[half, 0, 0], half, 1, 3, up).start()
        arrived(1, half)
        along(rows.at[half, 1, 0], half, 0, 3, down).start()

    def took(half, role, slot):
        wait_for(rows.at[half, role, slot], y_recv.at[half, role, slot - 1])

    def group_at(step):
        return pl.ds((plane + step) % groups * GROUP, GROUP)

    def exchange_far(piece):
        for role, rep in ((0, up), (1, down)):
            remote(rows.at[1, role, 0, group_at(far_planes[piece])], rows.at[1, 1 - role, 3, far_pieces[piece]],
                   p_send.at[role, piece], p_recv.at[1 - role, piece], rep, w).start()

    def exchange_near(stretch):
        for role, rep in ((0, up), (1, down)):
            remote(rows.at[1, role, 0, group_at(0), :, stretches[stretch]], rows.at[1, 1 - role, 3, near, :, stretches[stretch]],
                   p_send.at[role, 3 + stretch], p_recv.at[1 - role, 3 + stretch], rep, w).start()

    def product(left, half, role):
        return lax.dot_general(left, cols[half, role], (((1,), (1,)), ((), ())), preferred_element_type=jnp.float32)

    def multiply(half, role, slot):
        left = rows[half, role, slot].reshape(members * owned, depth)
        part[half, role, :, slot] = product(left, half, role).reshape(members, owned, 2 * cuts)

    def multiply_far(piece):
        at = far_pieces[piece]
        for role in range(2):
            wait_for(rows.at[1, role, 3, at], p_recv.at[role, piece])
            left = rows[1, role, 3, at].reshape(at.size * owned, depth)
            part[1, role, at, 3] = product(left, 1, role).reshape(at.size, owned, 2 * cuts)

    def multiply_near(role, stretch):
        inner = stretches[stretch]
        wait_for(rows.at[1, role, 3, near, :, inner], p_recv.at[role, 3 + stretch])
        left = rows[1, role, 3, near, :, inner].reshape(GROUP * owned, inner.size)
        some = lax.dot_general(
            left, cols[1, role, :, inner], (((1,), (1,)), ((), ())), preferred_element_type=jnp.float32
        ).reshape(GROUP, owned, 2 * cuts)
        part[1, role, near, 3] = some if stretch == 0 else part[1, role, near, 3] + some

    stages = (pl.ds(0, 2), pl.ds(2, 1), pl.ds(3, 1))

    def give(half, stage):
        slots, send, recv = stages[stage], r_send.at[half, stage], r_recv.at[half, stage]
        pltpu.make_async_copy(part.at[half, :, w, slots], landed.at[half, :, w, slots], recv).start()

        def one(t, carry):
            remote(
                part.at[half, :, other(t), slots], landed.at[half, :, w, slots], send, recv, r, other(t)
            ).start()
            return carry

        lax.fori_loop(1, members, one, 0)

    def give_far(piece):
        place, base = far_pieces[piece].start, (plane + far_planes[piece]) % groups * GROUP

        def one(t, carry):
            there = (seat + t) % GROUP
            remote(part.at[1, :, place + there, 3], landed.at[1, :, place + seat, 3], l_send, l_recv,
                   r, base + there).start()
            return carry

        lax.fori_loop(0, GROUP, one, 0)

    def give_direct(role, place, step, kept):
        base = (plane + step) % groups * GROUP

        def one(t, carry):
            there = (seat + t) % GROUP
            remote(part.at[1, role, place * GROUP + there, 3], direct.at[role, kept, seat], d_send.at[role],
                   d_recv.at[role], beside[3][role], base + there).start()
            return carry

        lax.fori_loop(0, GROUP, one, 0)

    def add_up(half, stage):
        slots = stages[stage]
        wait_for(landed.at[half, :, :, slots], r_recv.at[half, stage])
        handed[half, :, slots] = jnp.sum(landed[half, :, :, slots], axis=1).astype(handed.dtype)
        for role in range(2):
            g = irrep(role, half)
            for slot in ((0, 1), (2,), (3,))[stage]:
                if slot == 0:
                    placed[g, role] = handed[half, role, 0]
                else:
                    remote(handed.at[half, role, slot], placed.at[g, role], o_send.at[half, role, slot - 1],
                           o_recv.at[half], beside[slot][role], w).start()

    def add_up_far():
        wait_for(landed.at[1, :, pl.ds(GROUP, 2 * GROUP), 3], l_recv)
        last[...] = jnp.sum(landed[1, :, pl.ds(GROUP, 2 * GROUP), 3], axis=1)
        for role in range(2):
            remote(last.at[role], late.at[role], o_send.at[1, role, 2], late_recv.at[role], beside[3][role], w).start()

    def finish(half):
        for p in range(reps):
            g = reps * half + p
            found = {}
            for role, beyond in ((0, reps - 1), (1, 1)):
                here = (p + role) % reps
                piece = placed[g, role].astype(jnp.float32)
                found[here] = piece[:, :cuts]
                found[(here + beyond) % reps] = piece[:, cuts:]
            out[g] = jnp.concatenate([found[q] for q in range(reps)], axis=1).astype(out.dtype)

    send_columns(0)
    send_columns(1)
    meet_plane()
    spread(3, 0)
    spread(2, 0)
    for half in range(halves):
        for role in range(2):
            own_columns(half, role).start()
    spread(3, 1)
    spread(2, 1)
    relay_rows(0)
    spread(0, 0)
    spread(1, 0)
    relay_rows(1)
    spread(0, 1)
    spread(1, 1)
    forward_rows(0)
    exchange_rows(0)

    columns_ready(0)
    for role in range(2):
        multiply(0, role, 0)
        multiply(0, role, 1)
    give(0, 0)
    forward_rows(1)
    arrived(0, 1)
    arrived(1, 1)
    add_up(0, 0)
    columns_ready(1)
    for role in range(2):
        multiply(1, role, 0)
        multiply(1, role, 1)
    give(1, 0)
    for role in range(2):
        took(0, role, 2)
        multiply(0, role, 2)
    give(0, 1)
    add_up(1, 0)
    for role in range(2):
        took(0, role, 3)
        multiply(0, role, 3)
    give(0, 2)
    add_up(0, 1)
    exchange_far(0)
    exchange_far(1)
    for role in range(2):
        took(1, role, 2)
        multiply(1, role, 2)
    give(1, 1)
    add_up(0, 2)
    exchange_far(2)
    exchange_near(0)
    exchange_near(1)
    some = pl.ds(1, members - 1)
    for half in range(halves):
        for role in range(2):
            wait_for(cols.at[half, role, theirs], b_send.at[half, role])
            wait_for(rows.at[half, role, 0], y_send.at[half, role, 0])
        for behind in range(reps):
            wait_for(relay.at[half, 0, some], a_send.at[half, behind])
        wait_for(landed.at[half, :, some, stages[0]], r_send.at[half, 0])
    for stage in (1, 2):
        wait_for(landed.at[0, :, some, stages[stage]], r_send.at[0, stage])
        for role in range(2):
            wait_for(rows.at[0, role, 0], y_send.at[0, role, stage])
    for piece in range(2):
        multiply_far(piece)
        give_far(piece)
    multiply_far(2)
    for role in range(2):
        give_direct(role, 3, 3, 1)
    for role in range(2):
        multiply_near(role, 0)
    for role in range(2):
        multiply_near(role, 1)
        give_direct(role, 0, 0, 0)
    add_up(1, 1)
    wait_for(placed.at[pl.ds(0, reps - 1)], o_recv.at[0])
    finish(0)
    add_up_far()
    for role in range(2):
        wait_for(rows.at[1, role, 0], y_send.at[1, role, 1])
        for index in range(3):
            wait_for(rows.at[1, role, 0, far_pieces[index]], p_send.at[role, index])
        for index in range(2):
            wait_for(rows.at[1, role, 0, near, :, stretches[index]], p_send.at[role, 3 + index])
        for slot in range(3):
            wait_for(handed.at[0, role, slot], o_send.at[0, role, slot])
        for slot in range(2):
            wait_for(handed.at[1, role, slot], o_send.at[1, role, slot])
    wait_for(landed.at[1, :, some, stages[1]], r_send.at[1, 1])
    wait_for(landed.at[1, :, pl.ds(GROUP, 2 * GROUP), 3], l_send)
    for role in range(2):
        wait_for(direct.at[role], d_send.at[role])
        wait_for(direct.at[role], d_recv.at[role])
        wait_for(last.at[role], o_send.at[1, role, 2])
    wait_for(placed.at[pl.ds(reps, reps - 2)], o_recv.at[1])
    for role, behind in ((0, 1), (1, 0)):
        wait_for(late.at[role], late_recv.at[role])
        placed[irrep(behind, 1), role] = (late[role] + jnp.sum(direct[role], axis=(0, 1))).astype(placed.dtype)
    finish(1)


def per_device(reps, members, amplitudes, integrals, live_pairs):
    irreps, blocks, owned, depth = amplitudes.shape
    cuts = integrals.shape[1]
    halves = irreps // reps
    dma = pltpu.SemaphoreType.DMA
    f32, bf16 = jnp.float32, jnp.bfloat16
    sums = pl.pallas_call(
        functools.partial(ladder_kernel, reps, members),
        out_shape=jax.ShapeDtypeStruct((irreps, owned, reps * cuts), bf16),
        in_specs=[pl.BlockSpec(memory_space=pl.ANY)] * 2,
        out_specs=pl.BlockSpec(memory_space=pltpu.VMEM),
        scratch_shapes=[
            pltpu.VMEM((halves, 2, 4, members, owned, depth), bf16),
            pltpu.VMEM((halves, 2, members, owned, depth), bf16),
            pltpu.VMEM((halves, 2, 2 * cuts, depth), bf16),
            pltpu.VMEM((halves, 2, members, 4, owned, 2 * cuts), f32),
            pltpu.VMEM((halves, 2, members, 4, owned, 2 * cuts), f32),
            pltpu.VMEM((halves, 2, 4, owned, 2 * cuts), bf16),
            pltpu.VMEM((irreps, 2, owned, 2 * cuts), bf16),
            pltpu.VMEM((2, owned, 2 * cuts), f32),
            pltpu.VMEM((2, owned, 2 * cuts), f32),
            pltpu.VMEM((2, 2, GROUP, owned, 2 * cuts), f32),
            dma((halves, 2)), dma((halves, 2)), dma((halves, 2)),
            dma((halves, 4)), dma((halves, 4)),
            dma((halves, 2, 3)), dma((halves, 2, 3)),
            dma((2, 5)), dma((2, 5)),
            dma((halves, 3)), dma((halves, 3)),
            dma, dma,
            dma((halves, 2, 3)), dma((halves,)),
            dma((2,)), dma((2,)), dma((2,)), pltpu.SemaphoreType.REGULAR((2,)),
        ],
        compiler_params=pltpu.CompilerParams(collective_id=0, has_side_effects=True, vmem_limit_bytes=52 * MIB),
        cost_estimate=pl.CostEstimate(
            flops=2 * irreps * owned * members * 4 * cuts * depth, bytes_accessed=26 * MIB, transcendentals=0
        ),
        name="ladder",
    )(amplitudes, integrals)
    sums, live_pairs = lax.optimization_barrier((sums, live_pairs))
    first = (lax.axis_index("rep") * members + lax.axis_index("wide")) * owned
    index = first + lax.broadcasted_iota(jnp.int32, sums.shape, 1)
    return jnp.where(index < live_pairs[:, None, None], sums, jnp.zeros_like(sums))


def solution(mesh):
    in_specs = (P(None, None, ("rep", "wide"), None), P(None, "rep", "wide"), P())
    out_specs = P(None, ("rep", "wide"), None)
    return jax.shard_map(
        functools.partial(per_device, mesh.shape["rep"], mesh.shape["wide"]),
        mesh=mesh, in_specs=in_specs, out_specs=out_specs, check_vma=False,
    )
```

```python
import functools

import jax
import jax.numpy as jnp
from jax import lax
from jax.experimental import pallas as pl
from jax.experimental.pallas import tpu as pltpu
from jax.sharding import PartitionSpec as P

MESH = pl.DeviceIdType.MESH
MIB = 2**20
GROUP = 8


def ladder_kernel(reps, members, amp, integ, out, rows, relay, cols, part, landed, handed, placed, last, late, direct,
                  b_send, b_recv, b_own, a_send, a_recv, y_send, y_recv, p_send, p_recv,
                  r_send, r_recv, l_send, l_recv, o_send, o_recv, d_send, d_recv, late_recv, ready):
    r, w = lax.axis_index("rep"), lax.axis_index("wide")
    up, down, across = (r + 1) % reps, (r + reps - 1) % reps, (r + 2) % reps
    groups = members // GROUP
    plane, seat = w // GROUP, w % GROUP
    cuts = integ.shape[1]
    owned, depth = amp.shape[2], amp.shape[3]
    halves = amp.shape[0] // reps
    beside = {1: (down, up), 2: (across, across), 3: (up, down)}

    def irrep(behind, half):
        return (r + reps - behind) % reps + reps * half

    def remote(src, dst, send, recv, rep, member):
        return pltpu.make_async_remote_copy(
            src_ref=src, dst_ref=dst, send_sem=send, recv_sem=recv, device_id=(rep, member), device_id_type=MESH
        )

    def wait_for(ref, sem):
        pltpu.make_async_copy(ref, ref, sem).wait()

    def other(t):
        return (w + t) % members

    barrier = pltpu.get_barrier_semaphore()

    def greet(rep, member):
        pl.semaphore_signal(barrier, inc=1, device_id=(rep, member), device_id_type=MESH)

    greet(up, w)
    greet(down, w)
    for t in range(1, GROUP):
        greet(r, plane * GROUP + (seat + t) % GROUP)

    def each_after(act):
        for step in range(1, groups):
            @pl.when(plane + step < groups)
            def _():
                act(w + step * GROUP)

    def each_before(act):
        for step in range(1, groups):
            @pl.when(plane >= step)
            def _():
                act(w - step * GROUP)

    def tell(sem):
        def one(member):
            pl.semaphore_signal(sem, inc=1, device_id=(r, member), device_id_type=MESH)

        return one

    each_after(functools.partial(greet, r))
    pl.semaphore_wait(barrier, GROUP + 1 + plane)

    def meet_plane():
        each_before(tell(ready.at[0]))

        @pl.when(plane < groups - 1)
        def _():
            pl.semaphore_wait(ready.at[0], groups - 1 - plane)

        each_after(tell(ready.at[1]))

        @pl.when(plane > 0)
        def _():
            pl.semaphore_wait(ready.at[1], plane)

    mine, theirs = pl.ds(0, cuts), pl.ds(cuts, cuts)
    near = pl.ds(0, GROUP)
    far_planes = (2, 1, 3)
    far_pieces = tuple(pl.ds((k + 1) * GROUP, GROUP) for k in range(3))
    stretches = pl.ds(0, depth * 7 // 10), pl.ds(depth * 7 // 10, depth * 3 // 10)

    def send_columns(half):
        remote(integ.at[irrep(3, half)], cols.at[half, 0, theirs], b_send.at[half, 0], b_recv.at[half, 0], up, w).start()
        remote(integ.at[irrep(2, half)], cols.at[half, 1, theirs], b_send.at[half, 1], b_recv.at[half, 1], down, w).start()

    def own_columns(half, role):
        return pltpu.make_async_copy(integ.at[irrep(role, half)], cols.at[half, role, mine], b_own.at[half, role])

    def columns_ready(half):
        for role in range(2):
            own_columns(half, role).wait()
            wait_for(cols.at[half, role, theirs], b_recv.at[half, role])

    def arriving(behind, half):
        return rows.at[half, behind, 0] if behind < 2 else relay.at[half, behind - 2]

    def spread(behind, half):
        g, target = irrep(behind, half), arriving(behind, half)
        send, recv = a_send.at[half, behind], a_recv.at[half, behind]
        pltpu.make_async_copy(amp.at[g, w], target.at[w], recv).start()

        def one(t, carry):
            remote(amp.at[g, other(t)], target.at[w], send, recv, r, other(t)).start()
            return carry

        lax.fori_loop(1, members, one, 0)

    def arrived(behind, half):
        wait_for(arriving(behind, half), a_recv.at[half, behind])

    def along(src, half, role, slot, rep):
        return remote(src, rows.at[half, role, slot], y_send.at[half, role, slot - 1], y_recv.at[half, role, slot - 1],
                      rep, w)

    def relay_rows(half):
        arrived(3, half)
        along(relay.at[half, 1], half, 0, 1, up).start()
        arrived(2, half)
        along(relay.at[half, 0], half, 1, 1, down).start()

    def forward_rows(half):
        took(half, 0, 1)
        along(rows.at[half, 0, 1], half, 1, 2, up).start()
        took(half, 1, 1)
        along(rows.at[half, 1, 1], half, 0, 2, down).start()

    def exchange_rows(half):
        arrived(0, half)
        along(rows.at[half, 0, 0], half, 1, 3, up).start()
        arrived(1, half)
        along(rows.at[half, 1, 0], half, 0, 3, down).start()

    def took(half, role, slot):
        wait_for(rows.at[half, role, slot], y_recv.at[half, role, slot - 1])

    def group_at(step):
        return pl.ds((plane + step) % groups * GROUP, GROUP)

    def exchange_far(piece):
        for role, rep in ((0, up), (1, down)):
            remote(rows.at[1, role, 0, group_at(far_planes[piece])], rows.at[1, 1 - role, 3, far_pieces[piece]],
                   p_send.at[role, piece], p_recv.at[1 - role, piece], rep, w).start()

    def exchange_near(stretch):
        for role, rep in ((0, up), (1, down)):
            remote(rows.at[1, role, 0, group_at(0), :, stretches[stretch]], rows.at[1, 1 - role, 3, near, :, stretches[stretch]],
                   p_send.at[role, 3 + stretch], p_recv.at[1 - role, 3 + stretch], rep, w).start()

    def product(left, half, role):
        return lax.dot_general(left, cols[half, role], (((1,), (1,)), ((), ())), preferred_element_type=jnp.float32)

    def multiply(half, role, slot):
        left = rows[half, role, slot].reshape(members * owned, depth)
        part[half, role, :, slot] = product(left, half, role).reshape(members, owned, 2 * cuts)

    def multiply_far(piece):
        at = far_pieces[piece]
        for role in range(2):
            wait_for(rows.at[1, role, 3, at], p_recv.at[role, piece])
            left = rows[1, role, 3, at].reshape(at.size * owned, depth)
            part[1, role, at, 3] = product(left, 1, role).reshape(at.size, owned, 2 * cuts)

    def multiply_near(role, stretch):
        inner = stretches[stretch]
        wait_for(rows.at[1, role, 3, near, :, inner], p_recv.at[role, 3 + stretch])
        left = rows[1, role, 3, near, :, inner].reshape(GROUP * owned, inner.size)
        some = lax.dot_general(
            left, cols[1, role, :, inner], (((1,), (1,)), ((), ())), preferred_element_type=jnp.float32
        ).reshape(GROUP, owned, 2 * cuts)
        part[1, role, near, 3] = some if stretch == 0 else part[1, role, near, 3] + some

    stages = (pl.ds(0, 2), pl.ds(2, 1), pl.ds(3, 1))

    def give(half, stage):
        slots, send, recv = stages[stage], r_send.at[half, stage], r_recv.at[half, stage]
        pltpu.make_async_copy(part.at[half, :, w, slots], landed.at[half, :, w, slots], recv).start()

        def one(t, carry):
            remote(
                part.at[half, :, other(t), slots], landed.at[half, :, w, slots], send, recv, r, other(t)
            ).start()
            return carry

        lax.fori_loop(1, members, one, 0)

    def give_far(piece):
        place, base = far_pieces[piece].start, (plane + far_planes[piece]) % groups * GROUP

        def one(t, carry):
            there = (seat + t) % GROUP
            remote(part.at[1, :, place + there, 3], landed.at[1, :, place + seat, 3], l_send, l_recv,
                   r, base + there).start()
            return carry

        lax.fori_loop(0, GROUP, one, 0)

    def give_direct(role, place, step, kept):
        base = (plane + step) % groups * GROUP

        def one(t, carry):
            there = (seat + t) % GROUP
            remote(part.at[1, role, place * GROUP + there, 3], direct.at[role, kept, seat], d_send.at[role],
                   d_recv.at[role], beside[3][role], base + there).start()
            return carry

        lax.fori_loop(0, GROUP, one, 0)

    def add_up(half, stage):
        slots = stages[stage]
        wait_for(landed.at[half, :, :, slots], r_recv.at[half, stage])
        handed[half, :, slots] = jnp.sum(landed[half, :, :, slots], axis=1).astype(handed.dtype)
        for role in range(2):
            g = irrep(role, half)
            for slot in ((0, 1), (2,), (3,))[stage]:
                if slot == 0:
                    placed[g, role] = handed[half, role, 0]
                else:
                    remote(handed.at[half, role, slot], placed.at[g, role], o_send.at[half, role, slot - 1],
                           o_recv.at[half], beside[slot][role], w).start()

    def add_up_far():
        wait_for(landed.at[1, :, pl.ds(GROUP, 2 * GROUP), 3], l_recv)
        last[...] = jnp.sum(landed[1, :, pl.ds(GROUP, 2 * GROUP), 3], axis=1)
        for role in range(2):
            remote(last.at[role], late.at[role], o_send.at[1, role, 2], late_recv.at[role], beside[3][role], w).start()

    def finish(half):
        for p in range(reps):
            g = reps * half + p
            found = {}
            for role, beyond in ((0, reps - 1), (1, 1)):
                here = (p + role) % reps
                piece = placed[g, role].astype(jnp.float32)
                found[here] = piece[:, :cuts]
                found[(here + beyond) % reps] = piece[:, cuts:]
            out[g] = jnp.concatenate([found[q] for q in range(reps)], axis=1).astype(out.dtype)

    send_columns(0)
    send_columns(1)
    meet_plane()
    spread(3, 0)
    spread(2, 0)
    for half in range(halves):
        for role in range(2):
            own_columns(half, role).start()
    spread(3, 1)
    spread(2, 1)
    relay_rows(0)
    spread(0, 0)
    spread(1, 0)
    relay_rows(1)
    spread(0, 1)
    spread(1, 1)
    forward_rows(0)
    exchange_rows(0)

    columns_ready(0)
    for role in range(2):
        multiply(0, role, 0)
        multiply(0, role, 1)
    give(0, 0)
    forward_rows(1)
    arrived(0, 1)
    arrived(1, 1)
    add_up(0, 0)
    columns_ready(1)
    for role in range(2):
        multiply(1, role, 0)
        multiply(1, role, 1)
    give(1, 0)
    for role in range(2):
        took(0, role, 2)
        multiply(0, role, 2)
    give(0, 1)
    add_up(1, 0)
    for role in range(2):
        took(0, role, 3)
        multiply(0, role, 3)
    give(0, 2)
    add_up(0, 1)
    exchange_far(0)
    exchange_far(1)
    for role in range(2):
        took(1, role, 2)
        multiply(1, role, 2)
    give(1, 1)
    add_up(0, 2)
    exchange_far(2)
    exchange_near(0)
    exchange_near(1)
    some = pl.ds(1, members - 1)
    for half in range(halves):
        for role in range(2):
            wait_for(cols.at[half, role, theirs], b_send.at[half, role])
            wait_for(rows.at[half, role, 0], y_send.at[half, role, 0])
        for behind in range(reps):
            wait_for(relay.at[half, 0, some], a_send.at[half, behind])
        wait_for(landed.at[half, :, some, stages[0]], r_send.at[half, 0])
    for stage in (1, 2):
        wait_for(landed.at[0, :, some, stages[stage]], r_send.at[0, stage])
        for role in range(2):
            wait_for(rows.at[0, role, 0], y_send.at[0, role, stage])
    for piece in range(2):
        multiply_far(piece)
        give_far(piece)
    multiply_far(2)
    for role in range(2):
        give_direct(role, 3, 3, 1)
    for role in range(2):
        multiply_near(role, 0)
    for role in range(2):
        multiply_near(role, 1)
        give_direct(role, 0, 0, 0)
    add_up_far()
    add_up(1, 1)
    wait_for(placed.at[pl.ds(0, reps - 1)], o_recv.at[0])
    finish(0)
    for role in range(2):
        wait_for(rows.at[1, role, 0], y_send.at[1, role, 1])
        for index in range(3):
            wait_for(rows.at[1, role, 0, far_pieces[index]], p_send.at[role, index])
        for index in range(2):
            wait_for(rows.at[1, role, 0, near, :, stretches[index]], p_send.at[role, 3 + index])
        for slot in range(3):
            wait_for(handed.at[0, role, slot], o_send.at[0, role, slot])
        for slot in range(2):
            wait_for(handed.at[1, role, slot], o_send.at[1, role, slot])
    wait_for(landed.at[1, :, some, stages[1]], r_send.at[1, 1])
    wait_for(landed.at[1, :, pl.ds(GROUP, 2 * GROUP), 3], l_send)
    for role in range(2):
        wait_for(direct.at[role], d_send.at[role])
        wait_for(direct.at[role], d_recv.at[role])
        wait_for(last.at[role], o_send.at[1, role, 2])
    wait_for(placed.at[pl.ds(reps, reps - 2)], o_recv.at[1])
    for role, behind in ((0, 1), (1, 0)):
        wait_for(late.at[role], late_recv.at[role])
        placed[irrep(behind, 1), role] = (late[role] + jnp.sum(direct[role], axis=(0, 1))).astype(placed.dtype)
    finish(1)


def per_device(reps, members, amplitudes, integrals, live_pairs):
    irreps, blocks, owned, depth = amplitudes.shape
    cuts = integrals.shape[1]
    halves = irreps // reps
    dma = pltpu.SemaphoreType.DMA
    f32, bf16 = jnp.float32, jnp.bfloat16
    sums = pl.pallas_call(
        functools.partial(ladder_kernel, reps, members),
        out_shape=jax.ShapeDtypeStruct((irreps, owned, reps * cuts), bf16),
        in_specs=[pl.BlockSpec(memory_space=pl.ANY)] * 2,
        out_specs=pl.BlockSpec(memory_space=pltpu.VMEM),
        scratch_shapes=[
            pltpu.VMEM((halves, 2, 4, members, owned, depth), bf16),
            pltpu.VMEM((halves, 2, members, owned, depth), bf16),
            pltpu.VMEM((halves, 2, 2 * cuts, depth), bf16),
            pltpu.VMEM((halves, 2, members, 4, owned, 2 * cuts), f32),
            pltpu.VMEM((halves, 2, members, 4, owned, 2 * cuts), f32),
            pltpu.VMEM((halves, 2, 4, owned, 2 * cuts), bf16),
            pltpu.VMEM((irreps, 2, owned, 2 * cuts), bf16),
            pltpu.VMEM((2, owned, 2 * cuts), f32),
            pltpu.VMEM((2, owned, 2 * cuts), f32),
            pltpu.VMEM((2, 2, GROUP, owned, 2 * cuts), f32),
            dma((halves, 2)), dma((halves, 2)), dma((halves, 2)),
            dma((halves, 4)), dma((halves, 4)),
            dma((halves, 2, 3)), dma((halves, 2, 3)),
            dma((2, 5)), dma((2, 5)),
            dma((halves, 3)), dma((halves, 3)),
            dma, dma,
            dma((halves, 2, 3)), dma((halves,)),
            dma((2,)), dma((2,)), dma((2,)), pltpu.SemaphoreType.REGULAR((2,)),
        ],
        compiler_params=pltpu.CompilerParams(collective_id=0, has_side_effects=True, vmem_limit_bytes=52 * MIB),
        cost_estimate=pl.CostEstimate(
            flops=2 * irreps * owned * members * 4 * cuts * depth, bytes_accessed=26 * MIB, transcendentals=0
        ),
        name="ladder",
    )(amplitudes, integrals)
    sums, live_pairs = lax.optimization_barrier((sums, live_pairs))
    first = (lax.axis_index("rep") * members + lax.axis_index("wide")) * owned
    index = first + lax.broadcasted_iota(jnp.int32, sums.shape, 1)
    return jnp.where(index < live_pairs[:, None, None], sums, jnp.zeros_like(sums))


def solution(mesh):
    in_specs = (P(None, None, ("rep", "wide"), None), P(None, "rep", "wide"), P())
    out_specs = P(None, ("rep", "wide"), None)
    return jax.shard_map(
        functools.partial(per_device, mesh.shape["rep"], mesh.shape["wide"]),
        mesh=mesh, in_specs=in_specs, out_specs=out_specs, check_vma=False,
    )
```
